128 devices in a mesh: lat: 8 (over x, core), lon: 16 (over y, z).
Axes of the slice: x: 4, y: 4, z: 4, core: 2. Of those that a mesh axis runs over, the one named last changes fastest.
Arguments:
- op_blocks: bfloat16 [16384, 128, 128], P(('lat', 'lon')), may hold values from -0.5 to 0.5
- innovations: bfloat16 [16384, 16, 128], P(('lat', 'lon')), may hold values from -6 to 6
- obs_tiles: int32 [16384], P(('lat', 'lon')), may hold values from 0 to 127, as said below
- col_blocks: int32 [16384], P(('lat', 'lon')), may hold values from 0 to 255
- time_slots: int32 [16384], P(('lat', 'lon')), may hold values from 0 to 3
- obs_count: int32 [128], P(('lat', 'lon')), may hold values from 96 to 128, as said below
- courant: float32 [5, 512, 8192], P(None, 'lat', 'lon'), may hold values from 0.05 to 0.3
- later_adjoint: float32 [16, 512, 8192], P(None, 'lat', 'lon'), may hold values from -6 to 6
Outputs:
- gradient: float32 [16, 512, 8192], P(None, 'lat', 'lon')
The draws below stay inside these ranges and needn't reach their ends.
Inputs may be any that keep to these rules, and one draw needn't show every extreme that they name: `obs_tiles`: tiles are numbered with the latitude tile slowest. Among the used blocks of one device at most 2 name one tile, and in every draw some tile is named exactly 2 times by the used blocks of every device. `obs_count`: some device uses all 128 of its blocks.
All inputs are finite; a program needn't handle non-finite values.
Results may differ from the reference program's by a relative error of at most 0.0003.
Values may be sent and summed in bfloat16 or wider, within the bound.
No kernel may reach another device: no remote copies, remote signals or barrier semaphores. Data moves between devices by JAX's collectives and lax.ppermute only.
A program may use at most 128 MiB of HBM per device.

```python
import jax
import jax.numpy as jnp
from jax import lax

BLK = 128
LEV = 16
CLAT = 64
CLON = 512
OB = 128
STEPS = 4
CAP = 2
BLOCKS = 16384
NLAT = 512
NLON = 8192
N_LAT = 8
N_LON = 16


def draw_obs_tiles(key, part):
    key = jax.random.fold_in(key, 11)
    device_total = N_LAT * N_LON
    busiest = jax.random.randint(jax.random.fold_in(key, 1), (), 0, device_total).astype(jnp.int32)
    leading_len = 3 * OB // 4

    def one_row(row_key):
        first, second, third = jax.random.split(row_key, 3)
        shuffled = jax.random.permutation(first, device_total - 1).astype(jnp.int32)
        others = shuffled + (shuffled >= busiest).astype(jnp.int32)
        pool = jax.random.permutation(second, jnp.repeat(others, CAP))
        remainder = pool[:OB - CAP]
        leading = jnp.concatenate([jnp.full((CAP,), busiest, jnp.int32), remainder[:leading_len - CAP]])
        leading = jax.random.permutation(third, leading)
        return jnp.concatenate([leading, remainder[leading_len - CAP:]])
    row_keys = jax.random.split(jax.random.fold_in(key, 2), device_total)
    return jax.vmap(one_row)(row_keys).reshape(-1).astype(jnp.int32)


def draw_obs_count(key, part):
    key = jax.random.fold_in(key, 23)
    device_total = N_LAT * N_LON
    drawn = jax.random.randint(jax.random.fold_in(key, 1), (device_total,), 3 * OB // 4, OB + 1)
    chosen = jax.random.randint(jax.random.fold_in(key, 2), (), 0, device_total)
    return jnp.where(jnp.arange(device_total) == chosen, OB, drawn).astype(jnp.int32)


def plant(values, stream_key, smallest, high):
    index_at = [jax.random.randint(jax.random.fold_in(stream_key, axis), (), 0, length) for axis, length in enumerate(values.shape)]
    main_axis = values.shape.index(max(values.shape))
    next_to = index_at[:main_axis] + [(index_at[main_axis] + 1) % values.shape[main_axis]] + index_at[main_axis + 1:]
    return values.at[tuple(index_at)].set(smallest).at[tuple(next_to)].set(high)


def steps_of(rng, extent, pieces, low, largest):
    loudness, own = 1.0, jax.random.fold_in(rng, 6)
    for axis_at, blocks in pieces:
        steps = jnp.exp(jax.random.uniform(jax.random.fold_in(own, axis_at), (blocks,), jnp.float32, low / len(pieces), largest / len(pieces)))
        loudness = loudness * jnp.repeat(steps, extent[axis_at] // blocks).reshape([-1 if axis == axis_at else 1 for axis in range(len(extent))])
    return loudness


def bell_draw(stream_key, dims, width, most, pieces=(), dtype=jnp.bfloat16):
    level = steps_of(stream_key, dims, pieces, -0.22, 0.18) if pieces else 1.0
    values = jax.random.normal(stream_key, dims, jnp.float32) * width * level
    return jnp.minimum(jnp.maximum(values, -most), most).astype(dtype)


def setup_inputs(seed: int = 0) -> dict:
    splits = jax.random.split(jax.random.key(seed), 9)
    op_blocks = bell_draw(splits[0], (BLOCKS, BLK, BLK), BLK ** -0.5, 0.5, ((0, 128),))
    innovations = bell_draw(splits[1], (BLOCKS, LEV, BLK), 1.0, 6.0, ((0, 128),))
    obs_tiles = draw_obs_tiles(jax.random.fold_in(splits[8], 71), 0)
    col_blocks = plant(jax.random.randint(splits[3], (BLOCKS,), 0, CLAT * CLON // BLK), jax.random.fold_in(splits[3], 1), 0, (CLAT * CLON // BLK) - 1).astype(jnp.int32)
    time_slots = plant(jax.random.randint(splits[4], (BLOCKS,), 0, STEPS), jax.random.fold_in(splits[4], 1), 0, STEPS - 1).astype(jnp.int32)
    obs_count = draw_obs_count(jax.random.fold_in(splits[8], 71), 0)
    courant = jnp.clip(0.05 + 0.25 * jax.random.uniform(splits[6], (5, NLAT, NLON), jnp.float32) ** steps_of(splits[6], (5, NLAT, NLON), ((1, 8), (2, 16)), -0.2, 0.2), 0.05, 0.3)
    later_adjoint = bell_draw(splits[7], (LEV, NLAT, NLON), 1.0, 6.0, ((1, 8), (2, 16)), jnp.float32)
    return {"op_blocks": op_blocks, "innovations": innovations, "obs_tiles": obs_tiles, "col_blocks": col_blocks, "time_slots": time_slots, "obs_count": obs_count, "courant": courant, "later_adjoint": later_adjoint}


def with_rims(field):
    padded = jnp.pad(field, ((0, 0), (1, 1), (0, 0)))
    return jnp.concatenate([padded[:, :, -1:], padded, padded[:, :, :1]], axis=2)


def transpose_step(adjoint_state, center, neighbour):
    padded = with_rims(adjoint_state)
    result = center * adjoint_state
    result = result + neighbour[0, 1:-1, :-2] * padded[:, 1:-1, :-2]
    result = result + neighbour[1, 1:-1, 2:] * padded[:, 1:-1, 2:]
    result = result + neighbour[2, :-2, 1:-1] * padded[:, :-2, 1:-1]
    result = result + neighbour[3, 2:, 1:-1] * padded[:, 2:, 1:-1]
    return result


def reference(op_blocks, innovations, obs_tiles, col_blocks, time_slots, obs_count, courant, later_adjoint):
    device_total = N_LAT * N_LON
    column_blocks = CLAT * CLON // BLK
    usable = (jnp.arange(OB)[None, :] < obs_count[:, None]).reshape(-1).astype(jnp.float32)

    def contrib_of(operands):
        blocks_here, misfits = operands
        return jnp.einsum("blo,boc->blc", misfits.astype(jnp.float32), blocks_here.astype(jnp.float32),
                          precision=lax.Precision.HIGHEST)

    contrib = lax.map(contrib_of, (op_blocks.reshape(device_total, OB, BLK, BLK),
                                   innovations.reshape(device_total, OB, LEV, BLK)))
    contrib = contrib.reshape(device_total * OB, LEV, BLK) * usable[:, None, None]
    owner_rows = (obs_tiles * column_blocks + col_blocks).astype(jnp.int32)
    neighbour = with_rims(courant[1:])
    gradient = later_adjoint
    for slot_index in reversed(range(STEPS)):
        chosen = (time_slots == slot_index).astype(jnp.float32)
        tile_rows = jnp.zeros((device_total * column_blocks, LEV, BLK), jnp.float32)
        tile_rows = tile_rows.at[owner_rows].add(contrib * chosen[:, None, None])
        injected = tile_rows.reshape(N_LAT, N_LON, CLAT, CLON // BLK, LEV, BLK)
        injected = injected.transpose(4, 0, 2, 1, 3, 5).reshape(LEV, NLAT, NLON)
        gradient = transpose_step(gradient, courant[0], neighbour) + injected
    return gradient
```

```python
import jax
import jax.numpy as jnp
from jax import lax
from jax.experimental import pallas as pl
from jax.experimental.pallas import tpu as pltpu
from jax.sharding import PartitionSpec as P

STEPS = 4
LEV = 16
LANE = 128
NOTES = 2 * LEV
ROWS = NOTES + 8
PIECES = 4
OFFSETS = (0, 4, 9, 13)
HALO = 4
WEIGHTS = 5
PACK = 32
LIMIT = 32766.0
F32 = jnp.float32
I32 = jnp.int32
I16 = jnp.int16


def any_spec():
    return pl.BlockSpec(memory_space=pltpu.HBM)


def in_hbm(array):
    return pltpu.with_memory_space_constraint(array, pltpu.HBM)


def vmem_spec():
    return pl.BlockSpec(memory_space=pltpu.VMEM)


def params(mib):
    return pltpu.CompilerParams(vmem_limit_bytes=mib * 2**20)


def lanes8():
    return lax.broadcasted_iota(I32, (8, LANE), 1)


def sublanes8():
    return lax.broadcasted_iota(I32, (8, LANE), 0)


def aligned(index, by):
    return pl.multiple_of(index * by, by)


def log2_of(size):
    bits = size.bit_length() - 1
    assert size == 1 << bits
    return bits


def scale_of(code):
    return jnp.exp2(code * (1.0 / 16.0)) * (1.0 / LIMIT)


def shared_groups(value):
    value = value + pltpu.roll(value, 32, 1)
    return value + pltpu.roll(value, 64, 1)


def own_group():
    return lanes8() // 32 == sublanes8() % 4


def contribution_kernel(
    lat_cells, per_row, lon_tiles,
    count, tiles_hbm, cols_hbm, slots_hbm, op_hbm, inn_hbm, field_hbm, courant_hbm,
    sent, to_east, to_west,
    pay, op, inn, strip, meta, tiles, cols, slots, arrived, sems,
):
    blocks = op.shape[0]
    devices = lax.axis_size("lat") * lon_tiles
    parts = 4
    chunk = blocks // parts
    small = [
        pltpu.make_async_copy(a, b, sems.at[k])
        for k, (a, b) in enumerate(
            ((tiles_hbm, tiles), (cols_hbm, cols), (slots_hbm, slots))
        )
    ]
    inn_copy = pltpu.make_async_copy(inn_hbm, inn, sems.at[4])
    copies = []
    for part in range(parts):
        at = pl.ds(part * chunk, chunk)
        copies.append(pltpu.make_async_copy(op_hbm.at[at], op.at[at], sems.at[5 + part]))
    strips = []
    rows = field_hbm.shape[0]
    extra = courant_hbm.shape[0]
    for side, lane_at in enumerate((0, (per_row - 1) * LANE)):
        strips.append(
            pltpu.make_async_copy(
                field_hbm.at[:, pl.ds(lane_at, LANE)], strip.at[side, pl.ds(0, rows)],
                sems.at[5 + parts + 2 * side],
            )
        )
        strips.append(
            pltpu.make_async_copy(
                courant_hbm.at[:, pl.ds(lane_at, LANE)], strip.at[side, pl.ds(rows, extra)],
                sems.at[6 + parts + 2 * side],
            )
        )
    for copy in small + strips + [inn_copy] + copies:
        copy.start()

    def clear(d, _):
        arrived[d] = 0
        meta[pl.ds(aligned(d, 8), 8), :] = jnp.zeros((8, LANE), I32)
        return 0

    lax.fori_loop(0, devices + 1, clear, 0, unroll=8)
    lane8 = lanes8()
    lane = lane8[0:1]
    own = own_group()

    for copy in strips:
        copy.wait()
    total = (rows + extra) // 8
    for v in range(-(-total // PACK)):
        east = jnp.zeros((8, LANE), F32)
        west = jnp.zeros((8, LANE), F32)
        for k in range(min(PACK, total - v * PACK)):
            at = pl.ds(8 * (v * PACK + k), 8)
            here = lane8 // HALO == k
            west = jnp.where(here, pltpu.roll(strip[0, at, :], HALO * k, 1), west)
            east = jnp.where(here, pltpu.roll(strip[1, at, :], (HALO * k + HALO) % LANE, 1), east)
        to_east[pl.ds(8 * v, 8), :] = east
        to_west[pl.ds(8 * v, 8), :] = west

    for copy in small:
        copy.wait()
    used = count[0]
    me = lax.axis_index("lat") * lon_tiles + lax.axis_index("lon")
    seat = 8 * (me % 16)
    row_bits = log2_of(per_row)

    def one(j):
        repeat = jnp.where(j < used, 0, 1)
        j = jnp.minimum(j, used - 1)
        dest = tiles[j]
        col = cols[j]
        slot = slots[j]
        nth = jnp.minimum(arrived[dest] - repeat, 1)
        arrived[dest] = nth + 1
        row = col >> row_bits
        at_col = col & (per_row - 1)
        x = jnp.dot(inn[j], op[j], preferred_element_type=F32)
        largest = jnp.max(jnp.abs(x), axis=0, keepdims=True)
        code = jnp.floor(16.0 * jnp.log2(jnp.maximum(largest, 2.0**-100))) + 2.0
        q = jnp.round(x * (1.0 / scale_of(code)))
        pay[dest, pl.ds(pl.multiple_of(nth * LEV, LEV), LEV), :] = q.astype(I32).astype(I16)
        base = aligned(dest, 8)
        meta[pl.ds(base + nth, 1), :] = code.astype(I32)
        rim = (row < slot) | (row >= lat_cells - slot)
        target = (slot * lat_cells + row) * per_row + at_col + 1
        note = jnp.where(lane == seat + 6, 1, target)
        rim_seat = jnp.where(rim, seat + 6, LANE)
        pltpu.store(
            meta.at[pl.ds(base + 5, 1), :], note, mask=(lane == seat + nth) | (lane == rim_seat)
        )
        at_east = at_col == per_row - 1
        near = (at_east | (at_col == 0)) & (slot > 0)
        lon = dest & (lon_tiles - 1)
        other = jnp.where(at_east, lon + 1, lon + lon_tiles - 1) & (lon_tiles - 1)
        beside = jnp.where(near, dest - lon + other, devices)
        piece = nth + jnp.where(at_east, 2, 0)
        first = jnp.where(at_east, LANE - 3, 0)
        offset = jnp.where(at_east, 9, 0) + 4 * nth
        shift = (offset - first) & (LANE - 1)
        wanted = (lane8 >= first) & (lane8 < first + 3)
        mixed = pltpu.roll(jnp.where(wanted, q[:8], 0.0), shift, 1) + pltpu.roll(
            jnp.where(wanted, q[8:], 0.0), (shift + 16) & (LANE - 1), 1
        )
        mixed = jnp.where(own, shared_groups(mixed), 0.0)
        mixed = mixed + pltpu.roll(mixed, 1, 0)
        mixed = (mixed + pltpu.roll(mixed, 2, 0)).astype(I32)
        spot = lane & 15
        here = (spot >= offset) & (spot < offset + 3)
        base = aligned(beside, 8)
        pltpu.store(meta.at[pl.ds(base + 2, 1), :], mixed[3:4], mask=here)
        pltpu.store(meta.at[pl.ds(base + 3, 1), :], mixed[7:8], mask=here)
        turned = pltpu.roll(jnp.broadcast_to(code, (8, LANE)), shift, 1)[0:1].astype(I32)
        pltpu.store(meta.at[pl.ds(base + 4, 1), :], turned, mask=here & (lane < 16))
        note = jnp.where(lane >= seat + 6, 1, slot * lat_cells + row + 1)
        pltpu.store(
            meta.at[pl.ds(base + 5, 1), :], note,
            mask=(lane == seat + 2 + piece) | (lane == seat + 7) | (lane == rim_seat),
        )

    inn_copy.wait()
    for part in range(parts):
        copies[part].wait()

        def some(j, _):
            one(j)
            return 0

        lax.fori_loop(part * chunk, (part + 1) * chunk, some, 0, unroll=8)

    def settle(d, _):
        pay[d, pl.ds(NOTES, 8), :] = meta[pl.ds(aligned(d, 8), 8), :].astype(I16)
        return 0

    lax.fori_loop(0, devices, settle, 0, unroll=8)
    out_copy = pltpu.make_async_copy(pay, sent, sems.at[0])
    out_copy.start()
    out_copy.wait()


def contributions(op_blocks, innovations, obs_tiles, col_blocks, time_slots, obs_count, fields, courant, lat_cells, per_row, lon_tiles, devices):
    blocks = op_blocks.shape[0]
    packed = 8 * -(-(fields.shape[0] + courant.shape[0]) // (8 * PACK))
    strip_rows = fields.shape[0] + courant.shape[0]

    def kernel(*refs):
        contribution_kernel(lat_cells, per_row, lon_tiles, *refs)

    return pl.pallas_call(
        kernel,
        out_shape=[
            pltpu.HBM((devices, ROWS, LANE), I16),
            jax.ShapeDtypeStruct((packed, LANE), F32),
            jax.ShapeDtypeStruct((packed, LANE), F32),
        ],
        in_specs=[pl.BlockSpec(memory_space=pltpu.SMEM)] + [any_spec()] * 7,
        out_specs=[any_spec()] + [vmem_spec()] * 2,
        scratch_shapes=[
            pltpu.VMEM((devices, ROWS, LANE), I16),
            pltpu.VMEM(op_blocks.shape, op_blocks.dtype),
            pltpu.VMEM(innovations.shape, innovations.dtype),
            pltpu.VMEM((2, strip_rows, LANE), F32),
            pltpu.VMEM((8 * (devices + 1), LANE), I32),
            pltpu.SMEM(obs_tiles.shape, I32),
            pltpu.SMEM(col_blocks.shape, I32),
            pltpu.SMEM(time_slots.shape, I32),
            pltpu.SMEM((devices + 1,), I32),
            pltpu.SemaphoreType.DMA((13,)),
        ],
        compiler_params=params(16),
        cost_estimate=pl.CostEstimate(
            flops=2 * blocks * LEV * LANE * LANE, bytes_accessed=6 * 2**20, transcendentals=0
        ),
        name="contributions",
    )(
        obs_count, *map(in_hbm, (obs_tiles, col_blocks, time_slots, op_blocks, innovations, fields, courant))
    )


def ready_kernel(
    lat_cells, per_row, field_hbm, courant_hbm, first_hbm, spread_hbm, lat_hbm,
    first, spread, lat_rows, planes, cplanes, sems,
):
    copies = []
    for c in range(per_row):
        at = pl.ds(c * LANE, LANE)
        copies.append(pltpu.make_async_copy(field_hbm.at[:, at], planes.at[c], sems.at[2 * c]))
        copies.append(pltpu.make_async_copy(courant_hbm.at[:, at], cplanes.at[c], sems.at[2 * c + 1]))
    for copy in copies:
        copy.start()
    for copy in copies:
        copy.wait()

    def widen(g, _):
        for c in range(per_row):
            for d in range(WEIGHTS):
                eight = cplanes[c, pl.ds(pl.multiple_of(d * lat_cells + 8 * g, 8), 8), :]
                for k in range(8):
                    at = pl.ds(pl.multiple_of(((8 * g + k) * WEIGHTS + d) * 8, 8), 8)
                    spread[at, pl.ds(c * LANE, LANE)] = jnp.broadcast_to(eight[k : k + 1], (8, LANE))
        return 0

    lax.fori_loop(0, lat_cells // 8, widen, 0)
    spread_out = pltpu.make_async_copy(spread, spread_hbm.at[:, pl.ds(0, per_row * LANE)], sems.at[0])
    spread_out.start()
    parts = [(h, c) for h in range(LEV // 8) for c in range(per_row)]

    def row_of(i):
        return {
            (h, c): planes[c, pl.ds(8 * h * lat_cells + i, 8, stride=lat_cells), :] for h, c in parts
        }

    def finish(i, total, h, c):
        first[pl.ds(aligned(i, LEV) + 8 * h, 8), pl.ds(c * LANE, LANE)] = total

    for side, i in enumerate((0, lat_cells - 1)):
        row = row_of(i)
        for h, c in parts:
            lat_rows[pl.ds(LEV * side + 8 * h, 8), pl.ds(c * LANE, LANE)] = row[h, c]
    sweep(lat_cells, per_row, spread, row_of, None, finish, wrap=True)
    outs = [
        pltpu.make_async_copy(first, first_hbm, sems.at[1]),
        pltpu.make_async_copy(lat_rows, lat_hbm.at[:, pl.ds(0, per_row * LANE)], sems.at[2]),
    ]
    for out in outs:
        out.start()
    for out in outs + [spread_out]:
        out.wait()


def sweep(lat_cells, tiles, spread, row_of, force_of, finish, group_rows=8, wrap=False):
    lane = lanes8()
    parts = [(h, c) for h in range(LEV // 8) for c in range(tiles)]

    def weight_of(i, d):
        at = pl.ds(pl.multiple_of((i * WEIGHTS + d) * 8, 8), 8)
        return [spread[at, pl.ds(c * LANE, LANE)] for c in range(tiles)]

    def one_row(i, before, mine, after):
        center, east, west, south = (weight_of(i, d) for d in range(4))
        north = weight_of(i + 1, 4) if after is not None else None
        handed = {}
        for h in range(LEV // 8):
            up = [pltpu.roll(east[c] * mine[h, c], 1, 1) for c in range(tiles)]
            dn = [pltpu.roll(west[c] * mine[h, c], LANE - 1, 1) for c in range(tiles)]
            for c in range(tiles):
                total = center[c] * mine[h, c]
                left = 0.0 if wrap and c == 0 else up[c - 1]
                right = 0.0 if wrap and c == tiles - 1 else dn[(c + 1) % tiles]
                total = total + jnp.where(lane == 0, left, up[c])
                total = total + jnp.where(lane == LANE - 1, right, dn[c])
                if force_of is not None:
                    total = total + force_of(i, h, c)
                if before is not None:
                    total = total + before[h, c]
                if after is not None:
                    total = total + north[c] * after[h, c]
                handed[h, c] = south[c] * mine[h, c]
                finish(i, total, h, c)
            if wrap:
                seed = jnp.where(lane == 0, up[tiles - 1], jnp.where(lane == LANE - 1, dn[0], 0.0))
                finish(i, seed, h, tiles)
        return handed

    def rows(first, before, mine, number, ends):
        for k in range(number):
            after = None if ends and k == number - 1 else row_of(first + k + 1)
            before = one_row(first + k, before, mine, after)
            mine = after
        return before, mine

    def group(g, carry):
        before, mine = (dict(zip(parts, values)) for values in carry)
        before, mine = rows(g * group_rows, before, mine, group_rows, False)
        return tuple(before[p] for p in parts), tuple(mine[p] for p in parts)

    nothing = tuple(jnp.zeros((8, LANE), F32) for _ in parts)
    first = row_of(0)
    carry = lax.fori_loop(
        0, lat_cells // group_rows - 1, group, (nothing, tuple(first[p] for p in parts))
    )
    before, mine = (dict(zip(parts, values)) for values in carry)
    rows(lat_cells - group_rows, before, mine, group_rows, True)


def ready(fields, courant, lat_cells, per_row):
    wide = (per_row + 1) * LANE
    lon_cells = per_row * LANE

    def kernel(*refs):
        ready_kernel(lat_cells, per_row, *refs)

    return pl.pallas_call(
        kernel,
        out_shape=[
            pltpu.HBM((lat_cells * LEV, wide), F32),
            pltpu.HBM((lat_cells * WEIGHTS * 8, wide), F32),
            pltpu.HBM((2 * LEV, wide), F32),
        ],
        in_specs=[any_spec()] * 2,
        out_specs=[any_spec()] * 3,
        scratch_shapes=[
            pltpu.VMEM((lat_cells * LEV, wide), F32),
            pltpu.VMEM((lat_cells * WEIGHTS * 8, lon_cells), F32),
            pltpu.VMEM((2 * LEV, lon_cells), F32),
            pltpu.VMEM((per_row, fields.shape[0], LANE), F32),
            pltpu.VMEM((per_row, courant.shape[0], LANE), F32),
            pltpu.SemaphoreType.DMA((2 * per_row,)),
        ],
        compiler_params=params(16),
        cost_estimate=pl.CostEstimate(flops=10**7, bytes_accessed=12 * 2**20, transcendentals=0),
        name="first_step",
    )(in_hbm(fields), in_hbm(courant))


def place_kernel(
    lat_cells, per_row, got, east_halo, west_halo, first_hbm, spread_hbm, lat_hbm,
    force, south, north, lat_rows, spread,
    table_v, wrap_g, wrap_c, table, sems,
):
    wide = (per_row + 1) * LANE
    lon_cells = per_row * LANE
    sources = got.shape[0]
    row_bits = log2_of(per_row)
    top = (STEPS - 1) * lat_cells
    main = pl.ds(0, lon_cells)
    first_copy = pltpu.make_async_copy(first_hbm, force.at[pl.ds(top * LEV, lat_cells * LEV)], sems.at[0])
    lat_copy = pltpu.make_async_copy(lat_hbm.at[:, main], lat_rows.at[:, main], sems.at[1])
    spread_copy = pltpu.make_async_copy(spread_hbm.at[:, main], spread.at[:, main], sems.at[2])
    for copy in (first_copy, lat_copy, spread_copy):
        copy.start()
    for r in range(sources // 16):

        def gather(s, total, r=r):
            return total + got[16 * r + s, pl.ds(NOTES, 8), :].astype(I32)

        total = lax.fori_loop(0, 16, gather, jnp.zeros((8, LANE), I32), unroll=16)
        table_v[pl.ds(r, 1), :] = total[5:6]
    table_copy = pltpu.make_async_copy(table_v, table, sems.at[3])
    table_copy.start()

    def clear(r, _):
        force[pl.ds(aligned(r, LEV), LEV), :] = jnp.zeros((LEV, wide), F32)
        return 0

    lax.fori_loop(0, top, clear, 0, unroll=4)
    lane8 = lanes8()
    rows = wrap_g.shape[0] // 8
    extra = wrap_c.shape[0] // 8
    for n in range(rows + extra):
        v, k = divmod(n, PACK)
        at = pl.ds(8 * v, 8)
        low = pltpu.roll(east_halo[at, :], (-HALO * k) % LANE, 1)
        high = pltpu.roll(west_halo[at, :], (-HALO * k - HALO) % LANE, 1)
        wrap = jnp.where(lane8 < HALO, low, jnp.where(lane8 >= LANE - HALO, high, 0.0))
        if n < rows:
            wrap_g[pl.ds(8 * n, 8), :] = wrap
        else:
            wrap_c[pl.ds(8 * (n - rows), 8), :] = wrap
    last = pl.ds(lon_cells, LANE)
    for g in range(lat_cells // 8):
        for d in range(WEIGHTS):
            eight = wrap_c[pl.ds(d * lat_cells + 8 * g, 8), :]
            for k in range(8):
                spread[pl.ds(((8 * g + k) * WEIGHTS + d) * 8, 8), last] = jnp.broadcast_to(
                    eight[k : k + 1], (8, LANE)
                )
    first_copy.wait()

    def wrap_row(i, h):
        return wrap_g[pl.ds(8 * h * lat_cells + i, 8, stride=lat_cells), :]

    def weight(i, d):
        return spread[pl.ds(pl.multiple_of((i * WEIGHTS + d) * 8, 8), 8), last]

    def wrap_step(i, carry):
        center, east, west, south_w = (weight(i, d) for d in range(4))
        north_w = jnp.where(i < lat_cells - 1, weight(jnp.minimum(i + 1, lat_cells - 1), 4), 0.0)
        handed = []
        for h in range(LEV // 8):
            before, mine = carry[2 * h], carry[2 * h + 1]
            after = wrap_row(jnp.minimum(i + 1, lat_cells - 1), h)
            up = pltpu.roll(east * mine, 1, 1)
            dn = pltpu.roll(west * mine, LANE - 1, 1)
            at = pl.ds(aligned(top + i, LEV) + 8 * h, 8)
            total = center * mine + before + north_w * after
            total = total + jnp.where(lane8 == 0, 0.0, up) + jnp.where(lane8 == LANE - 1, 0.0, dn)
            force[at, last] = force[at, last] + total
            low = pl.ds(0, LANE)
            force[at, low] = force[at, low] + jnp.where(lane8 == 0, up, 0.0)
            high = pl.ds(lon_cells - LANE, LANE)
            force[at, high] = force[at, high] + jnp.where(lane8 == LANE - 1, dn, 0.0)
            handed += [south_w * mine, after]
        return tuple(handed)

    zero = jnp.zeros((8, LANE), F32)
    lax.fori_loop(0, lat_cells, wrap_step, (zero, wrap_row(0, 0), zero, wrap_row(0, 1)), unroll=4)
    for side, i in enumerate((0, lat_cells - 1)):
        for h in range(LEV // 8):
            lat_rows[pl.ds(LEV * side + 8 * h, 8), last] = wrap_row(i, h)
    table_copy.wait()
    lane8 = lanes8()
    dump = STEPS * lat_cells

    def entry(src, k):
        return table[src // 16, 8 * (src % 16) + k]

    def visit(src, _):
        q = got[src, pl.ds(0, NOTES), :].astype(I32).astype(F32)
        scales = scale_of(got[src, pl.ds(NOTES, 8), :].astype(I32).astype(F32))
        for nth in range(2):
            target = entry(src, nth)
            col = (target - 1) & (per_row - 1)
            row = jnp.where(target > 0, (target - 1) >> row_bits, dump)
            at = pl.ds(aligned(row, LEV), LEV)
            lanes = pl.ds(aligned(col, LANE), LANE)
            value = q[LEV * nth : LEV * nth + LEV] * scales[nth : nth + 1]
            force[at, lanes] = force[at, lanes] + value
        return 0

    lax.fori_loop(0, sources, visit, 0, unroll=8)
    own = own_group()
    in_low = (lane8 < 3)
    in_high = (lane8 >= LANE - 3)
    lanes = pl.ds(wide - LANE, LANE)

    def beside(src, _):
        @pl.when(entry(src, 7) > 0)
        def _():
            notes = got[src, pl.ds(NOTES, 8), :].astype(I32).astype(F32)
            base = jnp.broadcast_to(scale_of(notes[4:5]), (8, LANE))
            base = jnp.where(lane8 < 8, base, pltpu.roll(base, LANE - 16, 1))
            q = jnp.where(
                sublanes8() < 4,
                jnp.broadcast_to(notes[2:3], (8, LANE)),
                jnp.broadcast_to(notes[3:4], (8, LANE)),
            )
            q = shared_groups(jnp.where(own, q, 0.0))
            halves = [q * base, pltpu.roll(q, LANE - 16, 1) * base]
            for piece in range(PIECES):
                target = entry(src, 2 + piece)
                row = jnp.where(target > 0, target - 1, dump)
                at = aligned(row, LEV)
                for h, value in enumerate(halves if piece < 2 else halves[::-1]):
                    if piece == 1:
                        value = pltpu.roll(value, LANE - 4, 1)
                    if piece == 2:
                        value = pltpu.roll(value, 4, 1)
                    value = jnp.where(in_low if piece < 2 else in_high, value, 0.0)
                    where = pl.ds(at + 8 * h, 8)
                    force[where, lanes] = force[where, lanes] + value

        return 0

    lax.fori_loop(0, sources, beside, 0)
    lat_copy.wait()
    spread_copy.wait()
    n = 0
    for slot in (3, 2, 1):
        for d in range(slot):
            for side, (out, i) in enumerate(((south, lat_cells - 1 - d), (north, d))):
                out[pl.ds(LEV * n, LEV), :] = force[pl.ds((slot * lat_cells + i) * LEV, LEV), :]
            n += 1
    south[pl.ds(LEV * n, LEV), :] = lat_rows[pl.ds(LEV, LEV), :]
    north[pl.ds(LEV * n, LEV), :] = lat_rows[pl.ds(0, LEV), :]
    weight_at = LEV * (n + 1)
    sub = lax.broadcasted_iota(I32, (8, wide), 0)
    for d in range(3):
        for out, i in ((south, lat_cells - 1 - d), (north, d)):
            rows = jnp.zeros((8, wide), F32)
            for k in range(WEIGHTS):
                rows = jnp.where(sub == k, spread[pl.ds((i * WEIGHTS + k) * 8, 8), :], rows)
            out[pl.ds(weight_at + 8 * d, 8), :] = rows


def place(got, from_east, from_west, first, spread, lat_rows, fields, courant, lat_cells, per_row):
    wide = (per_row + 1) * LANE
    rim = (7 * LEV + 24, wide)

    def kernel(*refs):
        place_kernel(lat_cells, per_row, *refs)

    return pl.pallas_call(
        kernel,
        out_shape=[
            pltpu.VMEM(((STEPS * lat_cells + 1) * LEV, wide), F32),
            jax.ShapeDtypeStruct(rim, F32),
            jax.ShapeDtypeStruct(rim, F32),
            jax.ShapeDtypeStruct(lat_rows.shape, F32),
            pltpu.VMEM(spread.shape, F32),
        ],
        in_specs=[vmem_spec()] * 3 + [any_spec()] * 3,
        out_specs=[vmem_spec()] * 5,
        scratch_shapes=[
            pltpu.VMEM((8, LANE), I32),
            pltpu.VMEM((fields.shape[0], LANE), F32),
            pltpu.VMEM((courant.shape[0], LANE), F32),
            pltpu.SMEM((8, LANE), I32),
            pltpu.SemaphoreType.DMA((4,)),
        ],
        compiler_params=params(8),
        cost_estimate=pl.CostEstimate(flops=10**6, bytes_accessed=2 * 2**20, transcendentals=0),
        name="place_blocks",
    )(got, from_east, from_west, in_hbm(first), in_hbm(spread), in_hbm(lat_rows))


def steps_kernel(lat_cells, per_row, before, spread, force, out_hbm, result, sems):
    del before
    tiles = per_row + 1

    def at_of(slot, i, h):
        return pl.ds(pl.multiple_of((slot * lat_cells + i) * LEV, LEV) + 8 * h, 8)

    for slot in reversed(range(STEPS - 1)):

        def row_of(i, slot=slot):
            return {
                (h, c): force[at_of(slot + 1, i, h), pl.ds(c * LANE, LANE)]
                for h in range(LEV // 8)
                for c in range(tiles)
            }

        def force_of(i, h, c, slot=slot):
            return force[at_of(slot, i, h), pl.ds(c * LANE, LANE)]

        def finish(i, total, h, c, slot=slot):
            if slot or c < per_row:
                force[at_of(slot, i, h), pl.ds(c * LANE, LANE)] = total
            if slot == 0 and c < per_row:
                result[c, pl.ds(8 * h * lat_cells + i, 8, stride=lat_cells), :] = total

        sweep(lat_cells, tiles, spread, row_of, force_of, finish)
    writes = [
        pltpu.make_async_copy(result.at[c], out_hbm.at[:, pl.ds(c * LANE, LANE)], sems.at[c])
        for c in range(per_row)
    ]
    for write in writes:
        write.start()
    for write in writes:
        write.wait()


def steps(force, spread, lat_cells, per_row):
    lon_cells = per_row * LANE

    def kernel(*refs):
        steps_kernel(lat_cells, per_row, *refs)

    return pl.pallas_call(
        kernel,
        out_shape=[
            pltpu.VMEM(force.shape, F32),
            jax.ShapeDtypeStruct((LEV * lat_cells, lon_cells), F32),
        ],
        in_specs=[vmem_spec()] * 2,
        out_specs=[vmem_spec(), any_spec()],
        scratch_shapes=[
            pltpu.VMEM((per_row, LEV * lat_cells, LANE), F32),
            pltpu.SemaphoreType.DMA((per_row,)),
        ],
        input_output_aliases={0: 0},
        compiler_params=params(8),
        cost_estimate=pl.CostEstimate(
            flops=10 * STEPS * LEV * lat_cells * lon_cells, bytes_accessed=10 * 2**20, transcendentals=0
        ),
        name="interior_steps",
    )(force, spread)


def along_row(value, weights):
    wide = value.shape[1]
    return (
        weights[0] * value
        + pltpu.roll(weights[1] * value, 1, 1)
        + pltpu.roll(weights[2] * value, wide - 1, 1)
    )


def rim_kernel(
    lat_cells, per_row, before_hbm, from_north, from_south, force, lat_rows, spread, out_hbm, tiles, sems
):
    del before_hbm
    wide = force.shape[1]
    lon_cells = per_row * LANE
    weight_at = 7 * LEV
    writes = []
    for side, (halo, outer, inner) in enumerate(((from_north, 3, 4), (from_south, 4, 3))):

        def mine(q, side=side):
            return q if side == 0 else lat_cells - 1 - q

        def weight(q, d, halo=halo, mine=mine):
            if q < 0:
                row = halo[pl.ds(weight_at + 8 * (-1 - q), 8), :][d : d + 1]
                return jnp.broadcast_to(row, (LEV, wide))
            eight = spread[pl.ds((mine(q) * WEIGHTS + d) * 8, 8), :]
            return jnp.concatenate([eight, eight], axis=0)

        def sent(slot, q, halo=halo):
            first = {3: 0, 2: 3, 1: 5, 4: 6}[slot]
            return halo[pl.ds((first - 1 - q) * LEV, LEV), :]

        def inside(slot, q, side=side, mine=mine):
            if slot == STEPS:
                return lat_rows[pl.ds(LEV * side, LEV), :]
            return force[pl.ds((slot * lat_cells + mine(q)) * LEV, LEV), :]

        now = {}
        for step in range(1, STEPS + 1):
            slot = STEPS - step
            later = {}
            for q in range(-(STEPS - step), step):
                total = sent(slot, q) if q < 0 else None
                if step > 1 and q in now:
                    term = along_row(now[q], [weight(q, d) for d in range(3)])
                    total = term if total is None else total + term
                if step > 1 and q - 1 in now:
                    term = weight(q - 1, outer) * now[q - 1]
                    total = term if total is None else total + term
                if step == 1 and q == 0:
                    total = weight(-1, outer) * sent(STEPS, -1)
                if step > 1 and q + 1 in now:
                    total = total + weight(q + 1, inner) * now[q + 1]
                if q == -1:
                    total = total + weight(0, inner) * inside(slot + 1, 0)
                later[q] = total
            now = later
        for k in range(8):
            i = k if side == 0 else lat_cells - 8 + k
            row = force[pl.ds(i * LEV, LEV), pl.ds(0, lon_cells)]
            q = k if side == 0 else 7 - k
            if q < STEPS:
                row = row + now[q][:, :lon_cells]
            for c in range(per_row):
                tiles[side, c, pl.ds(k, LEV, stride=8), :] = row[:, c * LANE : (c + 1) * LANE]
        for c in range(per_row):
            write = pltpu.make_async_copy(
                tiles.at[side, c].reshape(LEV, 8, LANE),
                out_hbm.reshape(LEV, lat_cells, lon_cells).at[
                    :, pl.ds(0 if side == 0 else lat_cells - 8, 8), pl.ds(c * LANE, LANE)
                ],
                sems.at[per_row * side + c],
            )
            write.start()
            writes.append(write)
    for write in writes:
        write.wait()


def rim(result, from_north, from_south, force, lat_rows, spread, lat_cells, per_row):
    def kernel(*refs):
        rim_kernel(lat_cells, per_row, *refs)

    return pl.pallas_call(
        kernel,
        out_shape=jax.ShapeDtypeStruct(result.shape, F32),
        in_specs=[any_spec()] + [vmem_spec()] * 5,
        out_specs=any_spec(),
        scratch_shapes=[
            pltpu.VMEM((2, per_row, 8 * LEV, LANE), F32),
            pltpu.SemaphoreType.DMA((2 * per_row,)),
        ],
        input_output_aliases={0: 0},
        compiler_params=params(8),
        cost_estimate=pl.CostEstimate(flops=10**6, bytes_accessed=2 * 2**20, transcendentals=0),
        name="rim_rows",
    )(result, from_north, from_south, force, lat_rows, spread)


def on_device(
    op_blocks, innovations, obs_tiles, col_blocks, time_slots, obs_count, courant, later_adjoint
):
    lat_tiles = lax.axis_size("lat")
    lon_tiles = lax.axis_size("lon")
    devices = lat_tiles * lon_tiles
    levels, lat_cells, lon_cells = later_adjoint.shape
    per_row = lon_cells // LANE
    fields = later_adjoint.reshape(levels * lat_cells, lon_cells)
    weights = courant.reshape(courant.shape[0] * lat_cells, lon_cells)

    sent, to_east, to_west = contributions(
        op_blocks, innovations, obs_tiles, col_blocks, time_slots, obs_count,
        fields, weights, lat_cells, per_row, lon_tiles, devices,
    )
    eastward = [(i, (i + 1) % lon_tiles) for i in range(lon_tiles)]
    westward = [(j, i) for i, j in eastward]
    from_west = lax.ppermute(to_east, "lon", eastward)
    from_east = lax.ppermute(to_west, "lon", westward)
    got = lax.all_to_all(sent, ("lat", "lon"), split_axis=0, concat_axis=0, tiled=True)
    first, spread, lat_rows = ready(fields, weights, lat_cells, per_row)
    force, to_south, to_north, lat_rows, spread = place(
        got, from_east, from_west, first, spread, lat_rows, fields, weights, lat_cells, per_row
    )
    down = [(i, i + 1) for i in range(lat_tiles - 1)]
    up = [(j, i) for i, j in down]
    from_north = lax.ppermute(to_south, "lat", down)
    from_south = lax.ppermute(to_north, "lat", up)
    force, result = steps(force, spread, lat_cells, per_row)
    result = rim(result, from_north, from_south, force, lat_rows, spread, lat_cells, per_row)
    return result.reshape(levels, lat_cells, lon_cells)


def solution(mesh):
    in_specs = (
        P(("lat", "lon"), None, None),
        P(("lat", "lon"), None, None),
        P(("lat", "lon")),
        P(("lat", "lon")),
        P(("lat", "lon")),
        P(("lat", "lon")),
        P(None, "lat", "lon"),
        P(None, "lat", "lon"),
    )
    out_specs = P(None, "lat", "lon")
    return jax.shard_map(
        on_device, mesh=mesh, in_specs=in_specs, out_specs=out_specs, check_vma=False
    )
```

```python
import jax
import jax.numpy as jnp
from jax import lax
from jax.experimental import pallas as pl
from jax.experimental.pallas import tpu as pltpu
from jax.sharding import PartitionSpec as P

STEPS = 4
LEV = 16
LANE = 128
NOTES = 2 * LEV
ROWS = NOTES + 8
PIECES = 4
OFFSETS = (0, 4, 9, 13)
HALO = 4
WEIGHTS = 5
PACK = 32
LIMIT = 32766.0
F32 = jnp.float32
I32 = jnp.int32
I16 = jnp.int16


def any_spec():
    return pl.BlockSpec(memory_space=pltpu.HBM)


def in_hbm(array):
    return pltpu.with_memory_space_constraint(array, pltpu.HBM)


def vmem_spec():
    return pl.BlockSpec(memory_space=pltpu.VMEM)


def params(mib):
    return pltpu.CompilerParams(vmem_limit_bytes=mib * 2**20)


def lanes8():
    return lax.broadcasted_iota(I32, (8, LANE), 1)


def sublanes8():
    return lax.broadcasted_iota(I32, (8, LANE), 0)


def aligned(index, by):
    return pl.multiple_of(index * by, by)


def log2_of(size):
    bits = size.bit_length() - 1
    assert size == 1 << bits
    return bits


def scale_of(code):
    return jnp.exp2(code * (1.0 / 16.0)) * (1.0 / LIMIT)


def shared_groups(value):
    value = value + pltpu.roll(value, 32, 1)
    return value + pltpu.roll(value, 64, 1)


def own_group():
    return lanes8() // 32 == sublanes8() % 4


def contribution_kernel(
    lat_cells, per_row, lon_tiles,
    count, tiles_hbm, cols_hbm, slots_hbm, op_hbm, inn_hbm, field_hbm, courant_hbm,
    sent, to_east, to_west,
    pay, op, inn, strip, meta, tiles, cols, slots, arrived, sems,
):
    blocks = op.shape[0]
    devices = lax.axis_size("lat") * lon_tiles
    parts = 4
    chunk = blocks // parts
    small = [
        pltpu.make_async_copy(a, b, sems.at[k])
        for k, (a, b) in enumerate(
            ((tiles_hbm, tiles), (cols_hbm, cols), (slots_hbm, slots))
        )
    ]
    inn_copy = pltpu.make_async_copy(inn_hbm, inn, sems.at[4])
    copies = []
    for part in range(parts):
        at = pl.ds(part * chunk, chunk)
        copies.append(pltpu.make_async_copy(op_hbm.at[at], op.at[at], sems.at[5 + part]))
    strips = []
    rows = field_hbm.shape[0]
    extra = courant_hbm.shape[0]
    for side, lane_at in enumerate((0, (per_row - 1) * LANE)):
        strips.append(
            pltpu.make_async_copy(
                field_hbm.at[:, pl.ds(lane_at, LANE)], strip.at[side, pl.ds(0, rows)],
                sems.at[5 + parts + 2 * side],
            )
        )
        strips.append(
            pltpu.make_async_copy(
                courant_hbm.at[:, pl.ds(lane_at, LANE)], strip.at[side, pl.ds(rows, extra)],
                sems.at[6 + parts + 2 * side],
            )
        )
    for copy in small + strips + [inn_copy] + copies:
        copy.start()

    def clear(d, _):
        arrived[d] = 0
        meta[pl.ds(aligned(d, 8), 8), :] = jnp.zeros((8, LANE), I32)
        return 0

    lax.fori_loop(0, devices + 1, clear, 0, unroll=8)
    lane8 = lanes8()
    lane = lane8[0:1]
    own = own_group()

    for copy in strips:
        copy.wait()
    total = (rows + extra) // 8
    for v in range(-(-total // PACK)):
        east = jnp.zeros((8, LANE), F32)
        west = jnp.zeros((8, LANE), F32)
        for k in range(min(PACK, total - v * PACK)):
            at = pl.ds(8 * (v * PACK + k), 8)
            here = lane8 // HALO == k
            west = jnp.where(here, pltpu.roll(strip[0, at, :], HALO * k, 1), west)
            east = jnp.where(here, pltpu.roll(strip[1, at, :], (HALO * k + HALO) % LANE, 1), east)
        to_east[pl.ds(8 * v, 8), :] = east
        to_west[pl.ds(8 * v, 8), :] = west

    for copy in small:
        copy.wait()
    used = count[0]
    me = lax.axis_index("lat") * lon_tiles + lax.axis_index("lon")
    seat = 8 * (me % 16)
    row_bits = log2_of(per_row)

    def one(j):
        repeat = jnp.where(j < used, 0, 1)
        j = jnp.minimum(j, used - 1)
        dest = tiles[j]
        col = cols[j]
        slot = slots[j]
        nth = jnp.minimum(arrived[dest] - repeat, 1)
        arrived[dest] = nth + 1
        row = col >> row_bits
        at_col = col & (per_row - 1)
        x = jnp.dot(inn[j], op[j], preferred_element_type=F32)
        largest = jnp.max(jnp.abs(x), axis=0, keepdims=True)
        code = jnp.floor(16.0 * jnp.log2(jnp.maximum(largest, 2.0**-100))) + 2.0
        q = jnp.round(x * (1.0 / scale_of(code)))
        pay[dest, pl.ds(pl.multiple_of(nth * LEV, LEV), LEV), :] = q.astype(I32).astype(I16)
        base = aligned(dest, 8)
        meta[pl.ds(base + nth, 1), :] = code.astype(I32)
        rim = (row < slot) | (row >= lat_cells - slot)
        target = (slot * lat_cells + row) * per_row + at_col + 1
        note = jnp.where(lane == seat + 6, 1, target)
        rim_seat = jnp.where(rim, seat + 6, LANE)
        pltpu.store(
            meta.at[pl.ds(base + 5, 1), :], note, mask=(lane == seat + nth) | (lane == rim_seat)
        )
        at_east = at_col == per_row - 1
        near = (at_east | (at_col == 0)) & (slot > 0)
        lon = dest & (lon_tiles - 1)
        other = jnp.where(at_east, lon + 1, lon + lon_tiles - 1) & (lon_tiles - 1)
        beside = jnp.where(near, dest - lon + other, devices)
        piece = nth + jnp.where(at_east, 2, 0)
        first = jnp.where(at_east, LANE - 3, 0)
        offset = jnp.where(at_east, 9, 0) + 4 * nth
        shift = (offset - first) & (LANE - 1)
        wanted = (lane8 >= first) & (lane8 < first + 3)
        mixed = pltpu.roll(jnp.where(wanted, q[:8], 0.0), shift, 1) + pltpu.roll(
            jnp.where(wanted, q[8:], 0.0), (shift + 16) & (LANE - 1), 1
        )
        mixed = jnp.where(own, shared_groups(mixed), 0.0)
        mixed = mixed + pltpu.roll(mixed, 1, 0)
        mixed = (mixed + pltpu.roll(mixed, 2, 0)).astype(I32)
        spot = lane & 15
        here = (spot >= offset) & (spot < offset + 3)
        base = aligned(beside, 8)
        pltpu.store(meta.at[pl.ds(base + 2, 1), :], mixed[3:4], mask=here)
        pltpu.store(meta.at[pl.ds(base + 3, 1), :], mixed[7:8], mask=here)
        turned = pltpu.roll(jnp.broadcast_to(code, (8, LANE)), shift, 1)[0:1].astype(I32)
        pltpu.store(meta.at[pl.ds(base + 4, 1), :], turned, mask=here & (lane < 16))
        note = jnp.where(lane >= seat + 6, 1, slot * lat_cells + row + 1)
        pltpu.store(
            meta.at[pl.ds(base + 5, 1), :], note,
            mask=(lane == seat + 2 + piece) | (lane == seat + 7) | (lane == rim_seat),
        )

    inn_copy.wait()
    for part in range(parts):
        copies[part].wait()

        def some(j, _):
            one(j)
            return 0

        lax.fori_loop(part * chunk, (part + 1) * chunk, some, 0, unroll=32)

    def settle(d, _):
        pay[d, pl.ds(NOTES, 8), :] = meta[pl.ds(aligned(d, 8), 8), :].astype(I16)
        return 0

    lax.fori_loop(0, devices, settle, 0, unroll=8)
    out_copy = pltpu.make_async_copy(pay, sent, sems.at[0])
    out_copy.start()
    out_copy.wait()


def contributions(op_blocks, innovations, obs_tiles, col_blocks, time_slots, obs_count, fields, courant, lat_cells, per_row, lon_tiles, devices):
    blocks = op_blocks.shape[0]
    packed = 8 * -(-(fields.shape[0] + courant.shape[0]) // (8 * PACK))
    strip_rows = fields.shape[0] + courant.shape[0]

    def kernel(*refs):
        contribution_kernel(lat_cells, per_row, lon_tiles, *refs)

    return pl.pallas_call(
        kernel,
        out_shape=[
            pltpu.HBM((devices, ROWS, LANE), I16),
            jax.ShapeDtypeStruct((packed, LANE), F32),
            jax.ShapeDtypeStruct((packed, LANE), F32),
        ],
        in_specs=[pl.BlockSpec(memory_space=pltpu.SMEM)] + [any_spec()] * 7,
        out_specs=[any_spec()] + [vmem_spec()] * 2,
        scratch_shapes=[
            pltpu.VMEM((devices, ROWS, LANE), I16),
            pltpu.VMEM(op_blocks.shape, op_blocks.dtype),
            pltpu.VMEM(innovations.shape, innovations.dtype),
            pltpu.VMEM((2, strip_rows, LANE), F32),
            pltpu.VMEM((8 * (devices + 1), LANE), I32),
            pltpu.SMEM(obs_tiles.shape, I32),
            pltpu.SMEM(col_blocks.shape, I32),
            pltpu.SMEM(time_slots.shape, I32),
            pltpu.SMEM((devices + 1,), I32),
            pltpu.SemaphoreType.DMA((13,)),
        ],
        compiler_params=params(16),
        cost_estimate=pl.CostEstimate(
            flops=2 * blocks * LEV * LANE * LANE, bytes_accessed=6 * 2**20, transcendentals=0
        ),
        name="contributions",
    )(
        obs_count, *map(in_hbm, (obs_tiles, col_blocks, time_slots, op_blocks, innovations, fields, courant))
    )


def ready_kernel(
    lat_cells, per_row, field_hbm, courant_hbm, first_hbm, spread_hbm, lat_hbm,
    first, spread, lat_rows, planes, cplanes, sems,
):
    copies = []
    for c in range(per_row):
        at = pl.ds(c * LANE, LANE)
        copies.append(pltpu.make_async_copy(field_hbm.at[:, at], planes.at[c], sems.at[2 * c]))
        copies.append(pltpu.make_async_copy(courant_hbm.at[:, at], cplanes.at[c], sems.at[2 * c + 1]))
    for copy in copies:
        copy.start()
    for copy in copies:
        copy.wait()

    def widen(g, _):
        for c in range(per_row):
            for d in range(WEIGHTS):
                eight = cplanes[c, pl.ds(pl.multiple_of(d * lat_cells + 8 * g, 8), 8), :]
                for k in range(8):
                    at = pl.ds(pl.multiple_of(((8 * g + k) * WEIGHTS + d) * 8, 8), 8)
                    spread[at, pl.ds(c * LANE, LANE)] = jnp.broadcast_to(eight[k : k + 1], (8, LANE))
        return 0

    lax.fori_loop(0, lat_cells // 8, widen, 0)
    spread_out = pltpu.make_async_copy(spread, spread_hbm.at[:, pl.ds(0, per_row * LANE)], sems.at[0])
    spread_out.start()
    parts = [(h, c) for h in range(LEV // 8) for c in range(per_row)]

    def row_of(i):
        return {
            (h, c): planes[c, pl.ds(8 * h * lat_cells + i, 8, stride=lat_cells), :] for h, c in parts
        }

    def finish(i, total, h, c):
        first[pl.ds(aligned(i, LEV) + 8 * h, 8), pl.ds(c * LANE, LANE)] = total

    for side, i in enumerate((0, lat_cells - 1)):
        row = row_of(i)
        for h, c in parts:
            lat_rows[pl.ds(LEV * side + 8 * h, 8), pl.ds(c * LANE, LANE)] = row[h, c]
    sweep(lat_cells, per_row, spread, row_of, None, finish, wrap=True)
    outs = [
        pltpu.make_async_copy(first, first_hbm, sems.at[1]),
        pltpu.make_async_copy(lat_rows, lat_hbm.at[:, pl.ds(0, per_row * LANE)], sems.at[2]),
    ]
    for out in outs:
        out.start()
    for out in outs + [spread_out]:
        out.wait()


def sweep(lat_cells, tiles, spread, row_of, force_of, finish, wrap=False):
    lane = lanes8()
    parts = [(h, c) for h in range(LEV // 8) for c in range(tiles)]

    def weight_of(i, d):
        at = pl.ds(pl.multiple_of((i * WEIGHTS + d) * 8, 8), 8)
        return [spread[at, pl.ds(c * LANE, LANE)] for c in range(tiles)]

    def one_row(i, before, mine, after):
        center, east, west, south = (weight_of(i, d) for d in range(4))
        north = weight_of(i + 1, 4) if after is not None else None
        handed = {}
        for h in range(LEV // 8):
            up = [pltpu.roll(east[c] * mine[h, c], 1, 1) for c in range(tiles)]
            dn = [pltpu.roll(west[c] * mine[h, c], LANE - 1, 1) for c in range(tiles)]
            for c in range(tiles):
                total = center[c] * mine[h, c]
                left = 0.0 if wrap and c == 0 else up[c - 1]
                right = 0.0 if wrap and c == tiles - 1 else dn[(c + 1) % tiles]
                total = total + jnp.where(lane == 0, left, up[c])
                total = total + jnp.where(lane == LANE - 1, right, dn[c])
                if force_of is not None:
                    total = total + force_of(i, h, c)
                if before is not None:
                    total = total + before[h, c]
                if after is not None:
                    total = total + north[c] * after[h, c]
                handed[h, c] = south[c] * mine[h, c]
                finish(i, total, h, c)
            if wrap:
                seed = jnp.where(lane == 0, up[tiles - 1], jnp.where(lane == LANE - 1, dn[0], 0.0))
                finish(i, seed, h, tiles)
        return handed

    before, mine = None, row_of(0)
    for i in range(lat_cells):
        after = row_of(i + 1) if i + 1 < lat_cells else None
        before = one_row(i, before, mine, after)
        mine = after


def ready(fields, courant, lat_cells, per_row):
    wide = (per_row + 1) * LANE
    lon_cells = per_row * LANE

    def kernel(*refs):
        ready_kernel(lat_cells, per_row, *refs)

    return pl.pallas_call(
        kernel,
        out_shape=[
            pltpu.HBM((lat_cells * LEV, wide), F32),
            pltpu.HBM((lat_cells * WEIGHTS * 8, wide), F32),
            pltpu.HBM((2 * LEV, wide), F32),
        ],
        in_specs=[any_spec()] * 2,
        out_specs=[any_spec()] * 3,
        scratch_shapes=[
            pltpu.VMEM((lat_cells * LEV, wide), F32),
            pltpu.VMEM((lat_cells * WEIGHTS * 8, lon_cells), F32),
            pltpu.VMEM((2 * LEV, lon_cells), F32),
            pltpu.VMEM((per_row, fields.shape[0], LANE), F32),
            pltpu.VMEM((per_row, courant.shape[0], LANE), F32),
            pltpu.SemaphoreType.DMA((2 * per_row,)),
        ],
        compiler_params=params(16),
        cost_estimate=pl.CostEstimate(flops=10**7, bytes_accessed=12 * 2**20, transcendentals=0),
        name="first_step",
    )(in_hbm(fields), in_hbm(courant))


def place_kernel(
    lat_cells, per_row, got, east_halo, west_halo, first_hbm, spread_hbm, lat_hbm,
    force, south, north, lat_rows, spread,
    table_v, wrap_g, wrap_c, pieces, table, listed, sems,
):
    wide = (per_row + 1) * LANE
    lon_cells = per_row * LANE
    sources = got.shape[0]
    row_bits = log2_of(per_row)
    top = (STEPS - 1) * lat_cells
    main = pl.ds(0, lon_cells)
    first_copy = pltpu.make_async_copy(first_hbm, force.at[pl.ds(top * LEV, lat_cells * LEV)], sems.at[0])
    lat_copy = pltpu.make_async_copy(lat_hbm.at[:, main], lat_rows.at[:, main], sems.at[1])
    spread_copy = pltpu.make_async_copy(spread_hbm.at[:, main], spread.at[:, main], sems.at[2])
    for copy in (first_copy, lat_copy, spread_copy):
        copy.start()
    for r in range(sources // 16):

        def gather(s, total, r=r):
            return total + got[16 * r + s, pl.ds(NOTES, 8), :].astype(I32)

        total = lax.fori_loop(0, 16, gather, jnp.zeros((8, LANE), I32), unroll=16)
        table_v[pl.ds(r, 1), :] = total[5:6]
    table_copy = pltpu.make_async_copy(table_v, table, sems.at[3])
    table_copy.start()

    def clear(r, _):
        force[pl.ds(aligned(r, LEV), LEV), :] = jnp.zeros((LEV, wide), F32)
        return 0

    lax.fori_loop(0, top, clear, 0, unroll=4)
    lane8 = lanes8()
    rows = wrap_g.shape[0] // 8
    extra = wrap_c.shape[0] // 8
    for n in range(rows + extra):
        v, k = divmod(n, PACK)
        at = pl.ds(8 * v, 8)
        low = pltpu.roll(east_halo[at, :], (-HALO * k) % LANE, 1)
        high = pltpu.roll(west_halo[at, :], (-HALO * k - HALO) % LANE, 1)
        wrap = jnp.where(lane8 < HALO, low, jnp.where(lane8 >= LANE - HALO, high, 0.0))
        if n < rows:
            wrap_g[pl.ds(8 * n, 8), :] = wrap
        else:
            wrap_c[pl.ds(8 * (n - rows), 8), :] = wrap
    last = pl.ds(lon_cells, LANE)
    for g in range(lat_cells // 8):
        for d in range(WEIGHTS):
            eight = wrap_c[pl.ds(d * lat_cells + 8 * g, 8), :]
            for k in range(8):
                spread[pl.ds(((8 * g + k) * WEIGHTS + d) * 8, 8), last] = jnp.broadcast_to(
                    eight[k : k + 1], (8, LANE)
                )
    own = own_group()
    in_low = lane8 < 3
    in_high = lane8 >= LANE - 3

    def unpack(src, _):
        notes = got[src, pl.ds(NOTES, 8), :].astype(I32).astype(F32)
        base = jnp.broadcast_to(scale_of(notes[4:5]), (8, LANE))
        base = jnp.where(lane8 < 8, base, pltpu.roll(base, LANE - 16, 1))
        q = jnp.where(
            sublanes8() < 4,
            jnp.broadcast_to(notes[2:3], (8, LANE)),
            jnp.broadcast_to(notes[3:4], (8, LANE)),
        )
        q = shared_groups(jnp.where(own, q, 0.0))
        halves = [q * base, pltpu.roll(q, LANE - 16, 1) * base]
        for piece in range(PIECES):
            for h, value in enumerate(halves if piece < 2 else halves[::-1]):
                if piece == 1:
                    value = pltpu.roll(value, LANE - 4, 1)
                if piece == 2:
                    value = pltpu.roll(value, 4, 1)
                value = jnp.where(in_low if piece < 2 else in_high, value, 0.0)
                part = pl.ds(pl.multiple_of((src * PIECES + piece) * LEV, LEV) + 8 * h, 8)
                pieces[part, :] = value
        return 0

    lax.fori_loop(0, sources, unpack, 0, unroll=16)
    first_copy.wait()

    def wrap_row(i, h):
        return wrap_g[pl.ds(8 * h * lat_cells + i, 8, stride=lat_cells), :]

    def weight(i, d):
        return spread[pl.ds(pl.multiple_of((i * WEIGHTS + d) * 8, 8), 8), last]

    def wrap_step(i, carry):
        center, east, west, south_w = (weight(i, d) for d in range(4))
        north_w = jnp.where(i < lat_cells - 1, weight(jnp.minimum(i + 1, lat_cells - 1), 4), 0.0)
        handed = []
        for h in range(LEV // 8):
            before, mine = carry[2 * h], carry[2 * h + 1]
            after = wrap_row(jnp.minimum(i + 1, lat_cells - 1), h)
            up = pltpu.roll(east * mine, 1, 1)
            dn = pltpu.roll(west * mine, LANE - 1, 1)
            at = pl.ds(aligned(top + i, LEV) + 8 * h, 8)
            total = center * mine + before + north_w * after
            total = total + jnp.where(lane8 == 0, 0.0, up) + jnp.where(lane8 == LANE - 1, 0.0, dn)
            force[at, last] = force[at, last] + total
            low = pl.ds(0, LANE)
            force[at, low] = force[at, low] + jnp.where(lane8 == 0, up, 0.0)
            high = pl.ds(lon_cells - LANE, LANE)
            force[at, high] = force[at, high] + jnp.where(lane8 == LANE - 1, dn, 0.0)
            handed += [south_w * mine, after]
        return tuple(handed)

    zero = jnp.zeros((8, LANE), F32)
    lax.fori_loop(0, lat_cells, wrap_step, (zero, wrap_row(0, 0), zero, wrap_row(0, 1)), unroll=64)
    for side, i in enumerate((0, lat_cells - 1)):
        for h in range(LEV // 8):
            lat_rows[pl.ds(LEV * side + 8 * h, 8), last] = wrap_row(i, h)
    table_copy.wait()
    lane8 = lanes8()
    dump = STEPS * lat_cells

    last_lanes = pl.ds(wide - LANE, LANE)
    number = 0
    for src in range(sources):

        def entry(k, src=src):
            return table[src // 16, 8 * (src % 16) + k]

        q = got[src, pl.ds(0, NOTES), :].astype(I32).astype(F32)
        scales = scale_of(got[src, pl.ds(NOTES, 8), :].astype(I32).astype(F32))
        for nth in range(2):
            target = entry(nth)
            col = (target - 1) & (per_row - 1)
            row = jnp.where(target > 0, (target - 1) >> row_bits, dump)
            at = pl.ds(aligned(row, LEV), LEV)
            lanes = pl.ds(aligned(col, LANE), LANE)
            value = q[LEV * nth : LEV * nth + LEV] * scales[nth : nth + 1]
            force[at, lanes] = force[at, lanes] + value
        for piece in range(PIECES):
            target = entry(2 + piece)
            listed[number] = target + ((src * PIECES + piece) << 10)
            number = number + jnp.minimum(target, 1)
    for k in range(8):
        listed[number + k] = dump + 1

    def beside(group, _):
        for k in range(8):
            item = listed[8 * group + k]
            part = pl.ds(aligned(item >> 10, LEV), LEV)
            at = pl.ds(aligned((item & 1023) - 1, LEV), LEV)
            force[at, last_lanes] = force[at, last_lanes] + pieces[part, :]
        return 0

    lax.fori_loop(0, (number + 7) >> 3, beside, 0)
    lat_copy.wait()
    spread_copy.wait()
    n = 0
    for slot in (3, 2, 1):
        for d in range(slot):
            for side, (out, i) in enumerate(((south, lat_cells - 1 - d), (north, d))):
                out[pl.ds(LEV * n, LEV), :] = force[pl.ds((slot * lat_cells + i) * LEV, LEV), :]
            n += 1
    south[pl.ds(LEV * n, LEV), :] = lat_rows[pl.ds(LEV, LEV), :]
    north[pl.ds(LEV * n, LEV), :] = lat_rows[pl.ds(0, LEV), :]
    weight_at = LEV * (n + 1)
    sub = lax.broadcasted_iota(I32, (8, wide), 0)
    for d in range(3):
        for out, i in ((south, lat_cells - 1 - d), (north, d)):
            rows = jnp.zeros((8, wide), F32)
            for k in range(WEIGHTS):
                rows = jnp.where(sub == k, spread[pl.ds((i * WEIGHTS + k) * 8, 8), :], rows)
            out[pl.ds(weight_at + 8 * d, 8), :] = rows


def place(got, from_east, from_west, first, spread, lat_rows, fields, courant, lat_cells, per_row):
    wide = (per_row + 1) * LANE
    rim = (7 * LEV + 24, wide)

    def kernel(*refs):
        place_kernel(lat_cells, per_row, *refs)

    return pl.pallas_call(
        kernel,
        out_shape=[
            pltpu.VMEM(((STEPS * lat_cells + 1) * LEV, wide), F32),
            jax.ShapeDtypeStruct(rim, F32),
            jax.ShapeDtypeStruct(rim, F32),
            jax.ShapeDtypeStruct(lat_rows.shape, F32),
            pltpu.VMEM(spread.shape, F32),
        ],
        in_specs=[vmem_spec()] * 3 + [any_spec()] * 3,
        out_specs=[vmem_spec()] * 5,
        scratch_shapes=[
            pltpu.VMEM((8, LANE), I32),
            pltpu.VMEM((fields.shape[0], LANE), F32),
            pltpu.VMEM((courant.shape[0], LANE), F32),
            pltpu.VMEM((got.shape[0] * PIECES * LEV, LANE), F32),
            pltpu.SMEM((8, LANE), I32),
            pltpu.SMEM((got.shape[0] * PIECES + 8,), I32),
            pltpu.SemaphoreType.DMA((4,)),
        ],
        compiler_params=params(12),
        cost_estimate=pl.CostEstimate(flops=10**6, bytes_accessed=2 * 2**20, transcendentals=0),
        name="place_blocks",
    )(got, from_east, from_west, in_hbm(first), in_hbm(spread), in_hbm(lat_rows))


def steps_kernel(lat_cells, per_row, before, spread, force, out_hbm, result, sems):
    del before
    tiles = per_row + 1

    def at_of(slot, i, h):
        return pl.ds(pl.multiple_of((slot * lat_cells + i) * LEV, LEV) + 8 * h, 8)

    for slot in reversed(range(STEPS - 1)):

        def row_of(i, slot=slot):
            return {
                (h, c): force[at_of(slot + 1, i, h), pl.ds(c * LANE, LANE)]
                for h in range(LEV // 8)
                for c in range(tiles)
            }

        def force_of(i, h, c, slot=slot):
            return force[at_of(slot, i, h), pl.ds(c * LANE, LANE)]

        def finish(i, total, h, c, slot=slot):
            if slot or c < per_row:
                force[at_of(slot, i, h), pl.ds(c * LANE, LANE)] = total
            if slot == 0 and c < per_row:
                result[c, pl.ds(8 * h * lat_cells + i, 8, stride=lat_cells), :] = total

        sweep(lat_cells, tiles, spread, row_of, force_of, finish)
    writes = [
        pltpu.make_async_copy(result.at[c], out_hbm.at[:, pl.ds(c * LANE, LANE)], sems.at[c])
        for c in range(per_row)
    ]
    for write in writes:
        write.start()
    for write in writes:
        write.wait()


def steps(force, spread, lat_cells, per_row):
    lon_cells = per_row * LANE

    def kernel(*refs):
        steps_kernel(lat_cells, per_row, *refs)

    return pl.pallas_call(
        kernel,
        out_shape=[
            pltpu.VMEM(force.shape, F32),
            jax.ShapeDtypeStruct((LEV * lat_cells, lon_cells), F32),
        ],
        in_specs=[vmem_spec()] * 2,
        out_specs=[vmem_spec(), any_spec()],
        scratch_shapes=[
            pltpu.VMEM((per_row, LEV * lat_cells, LANE), F32),
            pltpu.SemaphoreType.DMA((per_row,)),
        ],
        input_output_aliases={0: 0},
        compiler_params=params(8),
        cost_estimate=pl.CostEstimate(
            flops=10 * STEPS * LEV * lat_cells * lon_cells, bytes_accessed=10 * 2**20, transcendentals=0
        ),
        name="interior_steps",
    )(force, spread)


def along_row(value, weights):
    wide = value.shape[1]
    return (
        weights[0] * value
        + pltpu.roll(weights[1] * value, 1, 1)
        + pltpu.roll(weights[2] * value, wide - 1, 1)
    )


def rim_kernel(
    lat_cells, per_row, before_hbm, from_north, from_south, force, lat_rows, spread, out_hbm, tiles, sems
):
    del before_hbm
    wide = force.shape[1]
    lon_cells = per_row * LANE
    weight_at = 7 * LEV
    writes = []
    for side, (halo, outer, inner) in enumerate(((from_north, 3, 4), (from_south, 4, 3))):

        def mine(q, side=side):
            return q if side == 0 else lat_cells - 1 - q

        def weight(q, d, halo=halo, mine=mine):
            if q < 0:
                row = halo[pl.ds(weight_at + 8 * (-1 - q), 8), :][d : d + 1]
                return jnp.broadcast_to(row, (LEV, wide))
            eight = spread[pl.ds((mine(q) * WEIGHTS + d) * 8, 8), :]
            return jnp.concatenate([eight, eight], axis=0)

        def sent(slot, q, halo=halo):
            first = {3: 0, 2: 3, 1: 5, 4: 6}[slot]
            return halo[pl.ds((first - 1 - q) * LEV, LEV), :]

        def inside(slot, q, side=side, mine=mine):
            if slot == STEPS:
                return lat_rows[pl.ds(LEV * side, LEV), :]
            return force[pl.ds((slot * lat_cells + mine(q)) * LEV, LEV), :]

        now = {}
        for step in range(1, STEPS + 1):
            slot = STEPS - step
            later = {}
            for q in range(-(STEPS - step), step):
                total = sent(slot, q) if q < 0 else None
                if step > 1 and q in now:
                    term = along_row(now[q], [weight(q, d) for d in range(3)])
                    total = term if total is None else total + term
                if step > 1 and q - 1 in now:
                    term = weight(q - 1, outer) * now[q - 1]
                    total = term if total is None else total + term
                if step == 1 and q == 0:
                    total = weight(-1, outer) * sent(STEPS, -1)
                if step > 1 and q + 1 in now:
                    total = total + weight(q + 1, inner) * now[q + 1]
                if q == -1:
                    total = total + weight(0, inner) * inside(slot + 1, 0)
                later[q] = total
            now = later
        for k in range(8):
            i = k if side == 0 else lat_cells - 8 + k
            row = force[pl.ds(i * LEV, LEV), pl.ds(0, lon_cells)]
            q = k if side == 0 else 7 - k
            if q < STEPS:
                row = row + now[q][:, :lon_cells]
            for c in range(per_row):
                tiles[side, c, pl.ds(k, LEV, stride=8), :] = row[:, c * LANE : (c + 1) * LANE]
        for c in range(per_row):
            write = pltpu.make_async_copy(
                tiles.at[side, c].reshape(LEV, 8, LANE),
                out_hbm.reshape(LEV, lat_cells, lon_cells).at[
                    :, pl.ds(0 if side == 0 else lat_cells - 8, 8), pl.ds(c * LANE, LANE)
                ],
                sems.at[per_row * side + c],
            )
            write.start()
            writes.append(write)
    for write in writes:
        write.wait()


def rim(result, from_north, from_south, force, lat_rows, spread, lat_cells, per_row):
    def kernel(*refs):
        rim_kernel(lat_cells, per_row, *refs)

    return pl.pallas_call(
        kernel,
        out_shape=jax.ShapeDtypeStruct(result.shape, F32),
        in_specs=[any_spec()] + [vmem_spec()] * 5,
        out_specs=any_spec(),
        scratch_shapes=[
            pltpu.VMEM((2, per_row, 8 * LEV, LANE), F32),
            pltpu.SemaphoreType.DMA((2 * per_row,)),
        ],
        input_output_aliases={0: 0},
        compiler_params=params(8),
        cost_estimate=pl.CostEstimate(flops=10**6, bytes_accessed=2 * 2**20, transcendentals=0),
        name="rim_rows",
    )(result, from_north, from_south, force, lat_rows, spread)


def on_device(
    op_blocks, innovations, obs_tiles, col_blocks, time_slots, obs_count, courant, later_adjoint
):
    lat_tiles = lax.axis_size("lat")
    lon_tiles = lax.axis_size("lon")
    devices = lat_tiles * lon_tiles
    levels, lat_cells, lon_cells = later_adjoint.shape
    per_row = lon_cells // LANE
    fields = later_adjoint.reshape(levels * lat_cells, lon_cells)
    weights = courant.reshape(courant.shape[0] * lat_cells, lon_cells)

    sent, to_east, to_west = contributions(
        op_blocks, innovations, obs_tiles, col_blocks, time_slots, obs_count,
        fields, weights, lat_cells, per_row, lon_tiles, devices,
    )
    eastward = [(i, (i + 1) % lon_tiles) for i in range(lon_tiles)]
    westward = [(j, i) for i, j in eastward]
    from_west = lax.ppermute(to_east, "lon", eastward)
    from_east = lax.ppermute(to_west, "lon", westward)
    got = lax.all_to_all(sent, ("lat", "lon"), split_axis=0, concat_axis=0, tiled=True)
    first, spread, lat_rows = ready(fields, weights, lat_cells, per_row)
    force, to_south, to_north, lat_rows, spread = place(
        got, from_east, from_west, first, spread, lat_rows, fields, weights, lat_cells, per_row
    )
    down = [(i, i + 1) for i in range(lat_tiles - 1)]
    up = [(j, i) for i, j in down]
    from_north = lax.ppermute(to_south, "lat", down)
    from_south = lax.ppermute(to_north, "lat", up)
    force, result = steps(force, spread, lat_cells, per_row)
    result = rim(result, from_north, from_south, force, lat_rows, spread, lat_cells, per_row)
    return result.reshape(levels, lat_cells, lon_cells)


def solution(mesh):
    in_specs = (
        P(("lat", "lon"), None, None),
        P(("lat", "lon"), None, None),
        P(("lat", "lon")),
        P(("lat", "lon")),
        P(("lat", "lon")),
        P(("lat", "lon")),
        P(None, "lat", "lon"),
        P(None, "lat", "lon"),
    )
    out_specs = P(None, "lat", "lon")
    return jax.shard_map(
        on_device, mesh=mesh, in_specs=in_specs, out_specs=out_specs, check_vma=False
    )
```

```python
import jax
import jax.numpy as jnp
from jax import lax
from jax.experimental import pallas as pl
from jax.experimental.pallas import tpu as pltpu
from jax.sharding import PartitionSpec as P

STEPS = 4
LEV = 16
LANE = 128
NOTES = 2 * LEV
ROWS = NOTES + 8
PIECES = 4
OFFSETS = (0, 4, 9, 13)
HALO = 4
WEIGHTS = 5
PACK = 32
LIMIT = 32766.0
F32 = jnp.float32
I32 = jnp.int32
I16 = jnp.int16


def any_spec():
    return pl.BlockSpec(memory_space=pltpu.HBM)


def in_hbm(array):
    return pltpu.with_memory_space_constraint(array, pltpu.HBM)


def vmem_spec():
    return pl.BlockSpec(memory_space=pltpu.VMEM)


def params(mib):
    return pltpu.CompilerParams(vmem_limit_bytes=mib * 2**20)


def lanes8():
    return lax.broadcasted_iota(I32, (8, LANE), 1)


def sublanes8():
    return lax.broadcasted_iota(I32, (8, LANE), 0)


def aligned(index, by):
    return pl.multiple_of(index * by, by)


def log2_of(size):
    bits = size.bit_length() - 1
    assert size == 1 << bits
    return bits


def scale_of(code):
    return jnp.exp2(code * (1.0 / 16.0)) * (1.0 / LIMIT)


def shared_groups(value):
    value = value + pltpu.roll(value, 32, 1)
    return value + pltpu.roll(value, 64, 1)


def own_group():
    return lanes8() // 32 == sublanes8() % 4


def contribution_kernel(
    lat_cells, per_row, lon_tiles,
    count, tiles_hbm, cols_hbm, slots_hbm, op_hbm, inn_hbm, field_hbm, courant_hbm,
    sent, to_east, to_west,
    pay, op, inn, strip, meta, tiles, cols, slots, arrived, sems,
):
    blocks = op.shape[0]
    devices = lax.axis_size("lat") * lon_tiles
    parts = 4
    chunk = blocks // parts
    small = [
        pltpu.make_async_copy(a, b, sems.at[k])
        for k, (a, b) in enumerate(
            ((tiles_hbm, tiles), (cols_hbm, cols), (slots_hbm, slots))
        )
    ]
    inn_copy = pltpu.make_async_copy(inn_hbm, inn, sems.at[4])
    copies = []
    for part in range(parts):
        at = pl.ds(part * chunk, chunk)
        copies.append(pltpu.make_async_copy(op_hbm.at[at], op.at[at], sems.at[5 + part]))
    strips = []
    rows = field_hbm.shape[0]
    extra = courant_hbm.shape[0]
    for side, lane_at in enumerate((0, (per_row - 1) * LANE)):
        strips.append(
            pltpu.make_async_copy(
                field_hbm.at[:, pl.ds(lane_at, LANE)], strip.at[side, pl.ds(0, rows)],
                sems.at[5 + parts + 2 * side],
            )
        )
        strips.append(
            pltpu.make_async_copy(
                courant_hbm.at[:, pl.ds(lane_at, LANE)], strip.at[side, pl.ds(rows, extra)],
                sems.at[6 + parts + 2 * side],
            )
        )
    for copy in small + [inn_copy] + copies + strips:
        copy.start()

    def clear(d, _):
        arrived[d] = 0
        meta[pl.ds(aligned(d, 8), 8), :] = jnp.zeros((8, LANE), I32)
        return 0

    lax.fori_loop(0, devices + 1, clear, 0, unroll=8)
    lane8 = lanes8()
    lane = lane8[0:1]
    own = own_group()

    for copy in small:
        copy.wait()
    used = count[0]
    me = lax.axis_index("lat") * lon_tiles + lax.axis_index("lon")
    seat = 8 * (me % 16)
    row_bits = log2_of(per_row)

    def one(j):
        repeat = jnp.where(j < used, 0, 1)
        j = jnp.minimum(j, used - 1)
        dest = tiles[j]
        col = cols[j]
        slot = slots[j]
        nth = jnp.minimum(arrived[dest] - repeat, 1)
        arrived[dest] = nth + 1
        row = col >> row_bits
        at_col = col & (per_row - 1)
        x = jnp.dot(inn[j], op[j], preferred_element_type=F32)
        largest = jnp.max(jnp.abs(x), axis=0, keepdims=True)
        code = jnp.floor(16.0 * jnp.log2(jnp.maximum(largest, 2.0**-100))) + 2.0
        q = jnp.round(x * (1.0 / scale_of(code)))
        pay[dest, pl.ds(pl.multiple_of(nth * LEV, LEV), LEV), :] = q.astype(I32).astype(I16)
        base = aligned(dest, 8)
        meta[pl.ds(base + nth, 1), :] = code.astype(I32)
        rim = (row < slot) | (row >= lat_cells - slot)
        target = (slot * lat_cells + row) * per_row + at_col + 1
        note = jnp.where(lane == seat + 6, 1, target)
        rim_seat = jnp.where(rim, seat + 6, LANE)
        pltpu.store(
            meta.at[pl.ds(base + 5, 1), :], note, mask=(lane == seat + nth) | (lane == rim_seat)
        )
        at_east = at_col == per_row - 1
        near = (at_east | (at_col == 0)) & (slot > 0)
        lon = dest & (lon_tiles - 1)
        other = jnp.where(at_east, lon + 1, lon + lon_tiles - 1) & (lon_tiles - 1)
        beside = jnp.where(near, dest - lon + other, devices)
        piece = nth + jnp.where(at_east, 2, 0)
        first = jnp.where(at_east, LANE - 3, 0)
        offset = jnp.where(at_east, 9, 0) + 4 * nth
        shift = (offset - first) & (LANE - 1)
        wanted = (lane8 >= first) & (lane8 < first + 3)
        mixed = pltpu.roll(jnp.where(wanted, q[:8], 0.0), shift, 1) + pltpu.roll(
            jnp.where(wanted, q[8:], 0.0), (shift + 16) & (LANE - 1), 1
        )
        mixed = jnp.where(own, shared_groups(mixed), 0.0)
        mixed = mixed + pltpu.roll(mixed, 1, 0)
        mixed = (mixed + pltpu.roll(mixed, 2, 0)).astype(I32)
        spot = lane & 15
        here = (spot >= offset) & (spot < offset + 3)
        base = aligned(beside, 8)
        pltpu.store(meta.at[pl.ds(base + 2, 1), :], mixed[3:4], mask=here)
        pltpu.store(meta.at[pl.ds(base + 3, 1), :], mixed[7:8], mask=here)
        turned = pltpu.roll(jnp.broadcast_to(code, (8, LANE)), shift, 1)[0:1].astype(I32)
        pltpu.store(meta.at[pl.ds(base + 4, 1), :], turned, mask=here & (lane < 16))
        note = jnp.where(lane >= seat + 6, 1, slot * lat_cells + row + 1)
        pltpu.store(
            meta.at[pl.ds(base + 5, 1), :], note,
            mask=(lane == seat + 2 + piece) | (lane == seat + 7) | (lane == rim_seat),
        )

    inn_copy.wait()
    for part in range(parts):
        copies[part].wait()

        def some(j, _):
            one(j)
            return 0

        lax.fori_loop(part * chunk, (part + 1) * chunk, some, 0, unroll=32)

    outs = []
    share = devices // parts
    for part in range(parts):

        def settle(d, _):
            pay[d, pl.ds(NOTES, 8), :] = meta[pl.ds(aligned(d, 8), 8), :].astype(I16)
            return 0

        lax.fori_loop(part * share, (part + 1) * share, settle, 0, unroll=share)
        at = pl.ds(part * share, share)
        outs.append(pltpu.make_async_copy(pay.at[at], sent.at[at], sems.at[part]))
        outs[-1].start()
    for copy in strips:
        copy.wait()
    total = (rows + extra) // 8
    for v in range(-(-total // PACK)):
        east = jnp.zeros((8, LANE), F32)
        west = jnp.zeros((8, LANE), F32)
        for k in range(min(PACK, total - v * PACK)):
            at = pl.ds(8 * (v * PACK + k), 8)
            group = lane8 // HALO
            west = jnp.where(group == k, pltpu.roll(strip[0, at, :], HALO * k, 1), west)
            east = jnp.where(group == (k - 1) % PACK, pltpu.roll(strip[1, at, :], HALO * k, 1), east)
        to_east[pl.ds(8 * v, 8), :] = east
        to_west[pl.ds(8 * v, 8), :] = west
    for out in outs:
        out.wait()


def contributions(op_blocks, innovations, obs_tiles, col_blocks, time_slots, obs_count, fields, courant, lat_cells, per_row, lon_tiles, devices):
    blocks = op_blocks.shape[0]
    packed = 8 * -(-(fields.shape[0] + courant.shape[0]) // (8 * PACK))
    strip_rows = fields.shape[0] + courant.shape[0]

    def kernel(*refs):
        contribution_kernel(lat_cells, per_row, lon_tiles, *refs)

    return pl.pallas_call(
        kernel,
        out_shape=[
            pltpu.HBM((devices, ROWS, LANE), I16),
            jax.ShapeDtypeStruct((packed, LANE), F32),
            jax.ShapeDtypeStruct((packed, LANE), F32),
        ],
        in_specs=[pl.BlockSpec(memory_space=pltpu.SMEM)] + [any_spec()] * 7,
        out_specs=[any_spec()] + [vmem_spec()] * 2,
        scratch_shapes=[
            pltpu.VMEM((devices, ROWS, LANE), I16),
            pltpu.VMEM(op_blocks.shape, op_blocks.dtype),
            pltpu.VMEM(innovations.shape, innovations.dtype),
            pltpu.VMEM((2, strip_rows, LANE), F32),
            pltpu.VMEM((8 * (devices + 1), LANE), I32),
            pltpu.SMEM(obs_tiles.shape, I32),
            pltpu.SMEM(col_blocks.shape, I32),
            pltpu.SMEM(time_slots.shape, I32),
            pltpu.SMEM((devices + 1,), I32),
            pltpu.SemaphoreType.DMA((13,)),
        ],
        compiler_params=params(16),
        cost_estimate=pl.CostEstimate(
            flops=2 * blocks * LEV * LANE * LANE, bytes_accessed=6 * 2**20, transcendentals=0
        ),
        name="contributions",
    )(
        obs_count, *map(in_hbm, (obs_tiles, col_blocks, time_slots, op_blocks, innovations, fields, courant))
    )


def ready_kernel(
    lat_cells, per_row, field_hbm, courant_hbm, first_hbm, spread_hbm, lat_hbm,
    first, spread, lat_rows, planes, cplanes, sems,
):
    copies = []
    for c in range(per_row):
        at = pl.ds(c * LANE, LANE)
        copies.append(pltpu.make_async_copy(field_hbm.at[:, at], planes.at[c], sems.at[2 * c]))
        copies.append(pltpu.make_async_copy(courant_hbm.at[:, at], cplanes.at[c], sems.at[2 * c + 1]))
    for copy in copies:
        copy.start()
    for copy in copies:
        copy.wait()

    def widen(g, _):
        for c in range(per_row):
            for d in range(WEIGHTS):
                eight = cplanes[c, pl.ds(pl.multiple_of(d * lat_cells + 8 * g, 8), 8), :]
                for k in range(8):
                    at = pl.ds(pl.multiple_of(((8 * g + k) * WEIGHTS + d) * 8, 8), 8)
                    spread[at, pl.ds(c * LANE, LANE)] = jnp.broadcast_to(eight[k : k + 1], (8, LANE))
        return 0

    lax.fori_loop(0, lat_cells // 8, widen, 0)
    spread_out = pltpu.make_async_copy(spread, spread_hbm.at[:, pl.ds(0, per_row * LANE)], sems.at[0])
    spread_out.start()
    parts = [(h, c) for h in range(LEV // 8) for c in range(per_row)]

    def row_of(i):
        return {
            (h, c): planes[c, pl.ds(8 * h * lat_cells + i, 8, stride=lat_cells), :] for h, c in parts
        }

    def finish(i, total, h, c):
        first[pl.ds(i * LEV + 8 * h, 8), pl.ds(c * LANE, LANE)] = total

    for side, i in enumerate((0, lat_cells - 1)):
        row = row_of(i)
        for h, c in parts:
            lat_rows[pl.ds(LEV * side + 8 * h, 8), pl.ds(c * LANE, LANE)] = row[h, c]
    sweep(lat_cells, per_row + 1, per_row, spread, row_of, None, finish)
    outs = [
        pltpu.make_async_copy(first, first_hbm, sems.at[1]),
        pltpu.make_async_copy(lat_rows, lat_hbm.at[:, pl.ds(0, per_row * LANE)], sems.at[2]),
    ]
    for out in outs:
        out.start()
    for out in outs + [spread_out]:
        out.wait()


def sweep(lat_cells, tiles, given, spread, row_of, force_of, finish, row_done=None):
    lane = lanes8()
    halves = range(LEV // 8)

    def weight_of(i, d):
        at = pl.ds((i * WEIGHTS + d) * 8, 8)
        return [spread[at, pl.ds(c * LANE, LANE)] for c in range(given)]

    def one_row(i, before, mine, after):
        center, east, west, south = (weight_of(i, d) for d in range(4))
        north = weight_of(i + 1, 4) if after is not None else None
        handed = {}
        for h in halves:
            up = [east[c] * mine[h, c] for c in range(given)]
            dn = [west[c] * mine[h, c] for c in range(given)]
            for c in range(tiles):
                if c == given:
                    total = jnp.where(lane == LANE - 1, up[c - 1], 0.0)
                    total = pltpu.roll(total, 1, 1)
                    other = jnp.where(lane == 0, dn[0], 0.0)
                    finish(i, total + pltpu.roll(other, LANE - 1, 1), h, c)
                    continue
                left = 0.0 if given < tiles and c == 0 else up[c - 1]
                right = 0.0 if given < tiles and c == given - 1 else dn[(c + 1) % given]
                total = center[c] * mine[h, c]
                total = total + pltpu.roll(jnp.where(lane == LANE - 1, left, up[c]), 1, 1)
                total = total + pltpu.roll(jnp.where(lane == 0, right, dn[c]), LANE - 1, 1)
                if force_of is not None:
                    total = total + force_of(i, h, c)
                if before is not None:
                    total = total + before[h, c]
                if after is not None:
                    total = total + north[c] * after[h, c]
                finish(i, total, h, c)
            for c in range(given):
                handed[h, c] = south[c] * mine[h, c]
        return handed

    before, mine = None, row_of(0)
    for i in range(lat_cells):
        after = row_of(i + 1) if i + 1 < lat_cells else None
        before = one_row(i, before, mine, after)
        mine = after
        if row_done is not None:
            row_done(i)


def ready(fields, courant, lat_cells, per_row):
    wide = (per_row + 1) * LANE
    lon_cells = per_row * LANE

    def kernel(*refs):
        ready_kernel(lat_cells, per_row, *refs)

    return pl.pallas_call(
        kernel,
        out_shape=[
            pltpu.HBM((lat_cells * LEV, wide), F32),
            pltpu.HBM((lat_cells * WEIGHTS * 8, wide), F32),
            pltpu.HBM((2 * LEV, wide), F32),
        ],
        in_specs=[any_spec()] * 2,
        out_specs=[any_spec()] * 3,
        scratch_shapes=[
            pltpu.VMEM((lat_cells * LEV, wide), F32),
            pltpu.VMEM((lat_cells * WEIGHTS * 8, lon_cells), F32),
            pltpu.VMEM((2 * LEV, lon_cells), F32),
            pltpu.VMEM((per_row, fields.shape[0], LANE), F32),
            pltpu.VMEM((per_row, courant.shape[0], LANE), F32),
            pltpu.SemaphoreType.DMA((2 * per_row,)),
        ],
        compiler_params=params(16),
        cost_estimate=pl.CostEstimate(flops=10**7, bytes_accessed=12 * 2**20, transcendentals=0),
        name="first_step",
    )(in_hbm(fields), in_hbm(courant))


def place_kernel(
    lat_cells, per_row, got, east_halo, west_halo, first_hbm, spread_hbm, lat_hbm,
    force, south, north, lat_rows, spread,
    table_v, wrap_g, wrap_c, pieces, table, listed, sems,
):
    wide = (per_row + 1) * LANE
    lon_cells = per_row * LANE
    sources = got.shape[0]
    row_bits = log2_of(per_row)
    top = (STEPS - 1) * lat_cells
    main = pl.ds(0, lon_cells)
    first_copy = pltpu.make_async_copy(first_hbm, force.at[pl.ds(top * LEV, lat_cells * LEV)], sems.at[0])
    lat_copy = pltpu.make_async_copy(lat_hbm.at[:, main], lat_rows.at[:, main], sems.at[1])
    spread_copy = pltpu.make_async_copy(spread_hbm.at[:, main], spread.at[:, main], sems.at[2])
    for copy in (first_copy, lat_copy, spread_copy):
        copy.start()
    for r in range(sources // 16):

        def gather(s, total, r=r):
            return total + got[16 * r + s, pl.ds(NOTES, 8), :].astype(I32)

        total = lax.fori_loop(0, 16, gather, jnp.zeros((8, LANE), I32), unroll=16)
        table_v[pl.ds(r, 1), :] = total[5:6]
    table_copy = pltpu.make_async_copy(table_v, table, sems.at[3])
    table_copy.start()

    def clear(r, _):
        force[pl.ds(aligned(r, LEV), LEV), :] = jnp.zeros((LEV, wide), F32)
        return 0

    lax.fori_loop(0, top, clear, 0, unroll=4)
    lane8 = lanes8()
    rows = wrap_g.shape[0] // 8
    extra = wrap_c.shape[0] // 8
    for n in range(rows + extra):
        v, k = divmod(n, PACK)
        at = pl.ds(8 * v, 8)
        both = jnp.where(lane8 // HALO == k, east_halo[at, :], west_halo[at, :])
        both = pltpu.roll(both, (-HALO * k) % LANE, 1)
        wrap = jnp.where((lane8 < HALO) | (lane8 >= LANE - HALO), both, 0.0)
        if n < rows:
            wrap_g[pl.ds(8 * n, 8), :] = wrap
        else:
            wrap_c[pl.ds(8 * (n - rows), 8), :] = wrap
    last = pl.ds(lon_cells, LANE)
    for g in range(lat_cells // 8):
        for d in range(WEIGHTS):
            eight = wrap_c[pl.ds(d * lat_cells + 8 * g, 8), :]
            for k in range(8):
                spread[pl.ds(((8 * g + k) * WEIGHTS + d) * 8, 8), last] = jnp.broadcast_to(
                    eight[k : k + 1], (8, LANE)
                )
    own = own_group()
    in_low = lane8 < 3
    in_high = lane8 >= LANE - 3

    def unpack(src, _):
        notes = got[src, pl.ds(NOTES, 8), :].astype(I32).astype(F32)
        base = jnp.broadcast_to(scale_of(notes[4:5]), (8, LANE))
        base = jnp.where(lane8 < 8, base, pltpu.roll(base, LANE - 16, 1))
        q = jnp.where(
            sublanes8() < 4,
            jnp.broadcast_to(notes[2:3], (8, LANE)),
            jnp.broadcast_to(notes[3:4], (8, LANE)),
        )
        q = shared_groups(jnp.where(own, q, 0.0))
        halves = [q * base, pltpu.roll(q, LANE - 16, 1) * base]
        for piece in range(PIECES):
            for h, value in enumerate(halves if piece < 2 else halves[::-1]):
                if piece == 1:
                    value = pltpu.roll(value, LANE - 4, 1)
                if piece == 2:
                    value = pltpu.roll(value, 4, 1)
                value = jnp.where(in_low if piece < 2 else in_high, value, 0.0)
                part = pl.ds(pl.multiple_of((src * PIECES + piece) * LEV, LEV) + 8 * h, 8)
                pieces[part, :] = value
        return 0

    lax.fori_loop(0, sources, unpack, 0, unroll=16)
    first_copy.wait()

    def wrap_row(i, h):
        return wrap_g[pl.ds(8 * h * lat_cells + i, 8, stride=lat_cells), :]

    def weight(i, d):
        return spread[pl.ds(pl.multiple_of((i * WEIGHTS + d) * 8, 8), 8), last]

    def wrap_step(i, carry):
        center, east, west, south_w = (weight(i, d) for d in range(4))
        north_w = jnp.where(i < lat_cells - 1, weight(jnp.minimum(i + 1, lat_cells - 1), 4), 0.0)
        handed = []
        for h in range(LEV // 8):
            before, mine = carry[2 * h], carry[2 * h + 1]
            after = wrap_row(jnp.minimum(i + 1, lat_cells - 1), h)
            up = pltpu.roll(east * mine, 1, 1)
            dn = pltpu.roll(west * mine, LANE - 1, 1)
            at = pl.ds(aligned(top + i, LEV) + 8 * h, 8)
            total = center * mine + before + north_w * after
            total = total + jnp.where(lane8 == 0, 0.0, up) + jnp.where(lane8 == LANE - 1, 0.0, dn)
            force[at, last] = force[at, last] + total
            low = pl.ds(0, LANE)
            force[at, low] = force[at, low] + jnp.where(lane8 == 0, up, 0.0)
            high = pl.ds(lon_cells - LANE, LANE)
            force[at, high] = force[at, high] + jnp.where(lane8 == LANE - 1, dn, 0.0)
            handed += [south_w * mine, after]
        return tuple(handed)

    zero = jnp.zeros((8, LANE), F32)
    lax.fori_loop(0, lat_cells, wrap_step, (zero, wrap_row(0, 0), zero, wrap_row(0, 1)), unroll=64)
    for side, i in enumerate((0, lat_cells - 1)):
        for h in range(LEV // 8):
            lat_rows[pl.ds(LEV * side + 8 * h, 8), last] = wrap_row(i, h)
    table_copy.wait()
    lane8 = lanes8()
    dump = STEPS * lat_cells

    last_lanes = pl.ds(wide - LANE, LANE)
    number = 0
    for src in range(sources):

        def entry(k, src=src):
            return table[src // 16, 8 * (src % 16) + k]

        q = got[src, pl.ds(0, NOTES), :].astype(I32).astype(F32)
        scales = scale_of(got[src, pl.ds(NOTES, 8), :].astype(I32).astype(F32))
        for nth in range(2):
            target = entry(nth)
            col = (target - 1) & (per_row - 1)
            row = jnp.where(target > 0, (target - 1) >> row_bits, dump)
            at = pl.ds(aligned(row, LEV), LEV)
            lanes = pl.ds(aligned(col, LANE), LANE)
            value = q[LEV * nth : LEV * nth + LEV] * scales[nth : nth + 1]
            force[at, lanes] = force[at, lanes] + value
        for piece in range(PIECES):
            target = entry(2 + piece)
            listed[number] = target + ((src * PIECES + piece) << 10)
            number = number + jnp.minimum(target, 1)
    for k in range(8):
        listed[number + k] = dump + 1

    def beside(group, _):
        for k in range(8):
            item = listed[8 * group + k]
            part = pl.ds(aligned(item >> 10, LEV), LEV)
            at = pl.ds(aligned((item & 1023) - 1, LEV), LEV)
            force[at, last_lanes] = force[at, last_lanes] + pieces[part, :]
        return 0

    lax.fori_loop(0, (number + 7) >> 3, beside, 0)
    lat_copy.wait()
    spread_copy.wait()
    n = 0
    for slot in (3, 2, 1):
        for d in range(slot):
            for side, (out, i) in enumerate(((south, lat_cells - 1 - d), (north, d))):
                out[pl.ds(LEV * n, LEV), :] = force[pl.ds((slot * lat_cells + i) * LEV, LEV), :]
            n += 1
    south[pl.ds(LEV * n, LEV), :] = lat_rows[pl.ds(LEV, LEV), :]
    north[pl.ds(LEV * n, LEV), :] = lat_rows[pl.ds(0, LEV), :]
    weight_at = LEV * (n + 1)
    sub = lax.broadcasted_iota(I32, (8, wide), 0)
    for d in range(3):
        for out, i in ((south, lat_cells - 1 - d), (north, d)):
            rows = jnp.zeros((8, wide), F32)
            for k in range(WEIGHTS):
                rows = jnp.where(sub == k, spread[pl.ds((i * WEIGHTS + k) * 8, 8), :], rows)
            out[pl.ds(weight_at + 8 * d, 8), :] = rows


def place(got, from_east, from_west, first, spread, lat_rows, fields, courant, lat_cells, per_row):
    wide = (per_row + 1) * LANE
    rim = (7 * LEV + 24, wide)

    def kernel(*refs):
        place_kernel(lat_cells, per_row, *refs)

    return pl.pallas_call(
        kernel,
        out_shape=[
            pltpu.VMEM(((STEPS * lat_cells + 1) * LEV, wide), F32),
            jax.ShapeDtypeStruct(rim, F32),
            jax.ShapeDtypeStruct(rim, F32),
            jax.ShapeDtypeStruct(lat_rows.shape, F32),
            pltpu.VMEM(spread.shape, F32),
        ],
        in_specs=[vmem_spec()] * 3 + [any_spec()] * 3,
        out_specs=[vmem_spec()] * 5,
        scratch_shapes=[
            pltpu.VMEM((8, LANE), I32),
            pltpu.VMEM((fields.shape[0], LANE), F32),
            pltpu.VMEM((courant.shape[0], LANE), F32),
            pltpu.VMEM((got.shape[0] * PIECES * LEV, LANE), F32),
            pltpu.SMEM((8, LANE), I32),
            pltpu.SMEM((got.shape[0] * PIECES + 8,), I32),
            pltpu.SemaphoreType.DMA((4,)),
        ],
        compiler_params=params(12),
        cost_estimate=pl.CostEstimate(flops=10**6, bytes_accessed=2 * 2**20, transcendentals=0),
        name="place_blocks",
    )(got, from_east, from_west, in_hbm(first), in_hbm(spread), in_hbm(lat_rows))


def steps_kernel(lat_cells, per_row, before, spread, force, out_hbm, result, sems):
    del before
    tiles = per_row + 1

    writes = []
    lon_cells = per_row * LANE
    out_rows = out_hbm.reshape(LEV, lat_cells, lon_cells)

    def at_of(slot, i, h):
        return pl.ds((slot * lat_cells + i) * LEV + 8 * h, 8)

    for slot in reversed(range(STEPS - 1)):

        def row_of(i, slot=slot):
            return {
                (h, c): force[at_of(slot + 1, i, h), pl.ds(c * LANE, LANE)]
                for h in range(LEV // 8)
                for c in range(tiles)
            }

        def force_of(i, h, c, slot=slot):
            return force[at_of(slot, i, h), pl.ds(c * LANE, LANE)]

        def finish(i, total, h, c, slot=slot):
            if slot or i < 8 or i >= lat_cells - 8:
                force[at_of(slot, i, h), pl.ds(c * LANE, LANE)] = total
            else:
                result[c, pl.ds(8 * h * lat_cells + i, 8, stride=lat_cells), :] = total

        def row_done(i):
            if i % 16 == 7 and i > 8:
                rows = pl.ds(i - 15, 16)
                for c in range(per_row):
                    write = pltpu.make_async_copy(
                        result.at[c].reshape(LEV, lat_cells, LANE).at[:, rows],
                        out_rows.at[:, rows, pl.ds(c * LANE, LANE)],
                        sems.at[len(writes)],
                    )
                    write.start()
                    writes.append(write)

        sweep(
            lat_cells, tiles if slot else per_row, tiles, spread, row_of, force_of, finish,
            None if slot else row_done,
        )
    for write in writes:
        write.wait()


def steps(force, spread, lat_cells, per_row):
    lon_cells = per_row * LANE

    def kernel(*refs):
        steps_kernel(lat_cells, per_row, *refs)

    return pl.pallas_call(
        kernel,
        out_shape=[
            pltpu.VMEM(force.shape, F32),
            jax.ShapeDtypeStruct((LEV * lat_cells, lon_cells), F32),
        ],
        in_specs=[vmem_spec()] * 2,
        out_specs=[vmem_spec(), any_spec()],
        scratch_shapes=[
            pltpu.VMEM((per_row, LEV * lat_cells, LANE), F32),
            pltpu.SemaphoreType.DMA((per_row * (lat_cells // 16),)),
        ],
        input_output_aliases={0: 0},
        compiler_params=params(8),
        cost_estimate=pl.CostEstimate(
            flops=10 * STEPS * LEV * lat_cells * lon_cells, bytes_accessed=10 * 2**20, transcendentals=0
        ),
        name="interior_steps",
    )(force, spread)


def along_row(value, weights):
    wide = value.shape[1]
    return (
        weights[0] * value
        + pltpu.roll(weights[1] * value, 1, 1)
        + pltpu.roll(weights[2] * value, wide - 1, 1)
    )


def rim_kernel(
    lat_cells, per_row, before_hbm, from_north, from_south, force, lat_rows, spread, out_hbm, tiles, sems
):
    del before_hbm
    wide = force.shape[1]
    lon_cells = per_row * LANE
    weight_at = 7 * LEV
    writes = []
    for side, (halo, outer, inner) in enumerate(((from_north, 3, 4), (from_south, 4, 3))):

        def mine(q, side=side):
            return q if side == 0 else lat_cells - 1 - q

        def weight(q, d, halo=halo, mine=mine):
            if q < 0:
                row = halo[pl.ds(weight_at + 8 * (-1 - q), 8), :][d : d + 1]
                return jnp.broadcast_to(row, (LEV, wide))
            eight = spread[pl.ds((mine(q) * WEIGHTS + d) * 8, 8), :]
            return jnp.concatenate([eight, eight], axis=0)

        def sent(slot, q, halo=halo):
            first = {3: 0, 2: 3, 1: 5, 4: 6}[slot]
            return halo[pl.ds((first - 1 - q) * LEV, LEV), :]

        def inside(slot, q, side=side, mine=mine):
            if slot == STEPS:
                return lat_rows[pl.ds(LEV * side, LEV), :]
            return force[pl.ds((slot * lat_cells + mine(q)) * LEV, LEV), :]

        now = {}
        for step in range(1, STEPS + 1):
            slot = STEPS - step
            later = {}
            for q in range(-(STEPS - step), step):
                total = sent(slot, q) if q < 0 else None
                if step > 1 and q in now:
                    term = along_row(now[q], [weight(q, d) for d in range(3)])
                    total = term if total is None else total + term
                if step > 1 and q - 1 in now:
                    term = weight(q - 1, outer) * now[q - 1]
                    total = term if total is None else total + term
                if step == 1 and q == 0:
                    total = weight(-1, outer) * sent(STEPS, -1)
                if step > 1 and q + 1 in now:
                    total = total + weight(q + 1, inner) * now[q + 1]
                if q == -1:
                    total = total + weight(0, inner) * inside(slot + 1, 0)
                later[q] = total
            now = later
        for k in range(8):
            i = k if side == 0 else lat_cells - 8 + k
            row = force[pl.ds(i * LEV, LEV), pl.ds(0, lon_cells)]
            q = k if side == 0 else 7 - k
            if q < STEPS:
                row = row + now[q][:, :lon_cells]
            for c in range(per_row):
                tiles[side, c, pl.ds(k, LEV, stride=8), :] = row[:, c * LANE : (c + 1) * LANE]
        for c in range(per_row):
            write = pltpu.make_async_copy(
                tiles.at[side, c].reshape(LEV, 8, LANE),
                out_hbm.reshape(LEV, lat_cells, lon_cells).at[
                    :, pl.ds(0 if side == 0 else lat_cells - 8, 8), pl.ds(c * LANE, LANE)
                ],
                sems.at[per_row * side + c],
            )
            write.start()
            writes.append(write)
    for write in writes:
        write.wait()


def rim(result, from_north, from_south, force, lat_rows, spread, lat_cells, per_row):
    def kernel(*refs):
        rim_kernel(lat_cells, per_row, *refs)

    return pl.pallas_call(
        kernel,
        out_shape=jax.ShapeDtypeStruct(result.shape, F32),
        in_specs=[any_spec()] + [vmem_spec()] * 5,
        out_specs=any_spec(),
        scratch_shapes=[
            pltpu.VMEM((2, per_row, 8 * LEV, LANE), F32),
            pltpu.SemaphoreType.DMA((2 * per_row,)),
        ],
        input_output_aliases={0: 0},
        compiler_params=params(8),
        cost_estimate=pl.CostEstimate(flops=10**6, bytes_accessed=2 * 2**20, transcendentals=0),
        name="rim_rows",
    )(result, from_north, from_south, force, lat_rows, spread)


def on_device(
    op_blocks, innovations, obs_tiles, col_blocks, time_slots, obs_count, courant, later_adjoint
):
    lat_tiles = lax.axis_size("lat")
    lon_tiles = lax.axis_size("lon")
    devices = lat_tiles * lon_tiles
    levels, lat_cells, lon_cells = later_adjoint.shape
    per_row = lon_cells // LANE
    fields = later_adjoint.reshape(levels * lat_cells, lon_cells)
    weights = courant.reshape(courant.shape[0] * lat_cells, lon_cells)

    sent, to_east, to_west = contributions(
        op_blocks, innovations, obs_tiles, col_blocks, time_slots, obs_count,
        fields, weights, lat_cells, per_row, lon_tiles, devices,
    )
    eastward = [(i, (i + 1) % lon_tiles) for i in range(lon_tiles)]
    westward = [(j, i) for i, j in eastward]
    from_west = lax.ppermute(to_east, "lon", eastward)
    from_east = lax.ppermute(to_west, "lon", westward)
    got = lax.all_to_all(sent, ("lat", "lon"), split_axis=0, concat_axis=0, tiled=True)
    first, spread, lat_rows = ready(fields, weights, lat_cells, per_row)
    force, to_south, to_north, lat_rows, spread = place(
        got, from_east, from_west, first, spread, lat_rows, fields, weights, lat_cells, per_row
    )
    down = [(i, i + 1) for i in range(lat_tiles - 1)]
    up = [(j, i) for i, j in down]
    from_north = lax.ppermute(to_south, "lat", down)
    from_south = lax.ppermute(to_north, "lat", up)
    force, result = steps(force, spread, lat_cells, per_row)
    result = rim(result, from_north, from_south, force, lat_rows, spread, lat_cells, per_row)
    return result.reshape(levels, lat_cells, lon_cells)


def solution(mesh):
    in_specs = (
        P(("lat", "lon"), None, None),
        P(("lat", "lon"), None, None),
        P(("lat", "lon")),
        P(("lat", "lon")),
        P(("lat", "lon")),
        P(("lat", "lon")),
        P(None, "lat", "lon"),
        P(None, "lat", "lon"),
    )
    out_specs = P(None, "lat", "lon")
    return jax.shard_map(
        on_device, mesh=mesh, in_specs=in_specs, out_specs=out_specs, check_vma=False
    )
```

```python
import jax
import jax.numpy as jnp
from jax import lax
from jax.experimental import pallas as pl
from jax.experimental.pallas import tpu as pltpu
from jax.sharding import PartitionSpec as P

STEPS = 4
LEV = 16
LANE = 128
NOTES = 2 * LEV
ROWS = NOTES + 8
PIECES = 4
OFFSETS = (0, 4, 9, 13)
HALO = 4
WEIGHTS = 5
PACK = 32
LIMIT = 32766.0
F32 = jnp.float32
I32 = jnp.int32
I16 = jnp.int16


def any_spec():
    return pl.BlockSpec(memory_space=pltpu.HBM)


def in_hbm(array):
    return pltpu.with_memory_space_constraint(array, pltpu.HBM)


def vmem_spec():
    return pl.BlockSpec(memory_space=pltpu.VMEM)


def params(mib):
    return pltpu.CompilerParams(vmem_limit_bytes=mib * 2**20)


def lanes8():
    return lax.broadcasted_iota(I32, (8, LANE), 1)


def sublanes8():
    return lax.broadcasted_iota(I32, (8, LANE), 0)


def aligned(index, by):
    return pl.multiple_of(index * by, by)


def log2_of(size):
    bits = size.bit_length() - 1
    assert size == 1 << bits
    return bits


def scale_of(code):
    return jnp.exp2(code * (1.0 / 16.0)) * (1.0 / LIMIT)


def shared_groups(value):
    value = value + pltpu.roll(value, 32, 1)
    return value + pltpu.roll(value, 64, 1)


def own_group():
    return lanes8() // 32 == sublanes8() % 4


def contribution_kernel(
    lat_cells, per_row, lon_tiles,
    count, tiles_hbm, cols_hbm, slots_hbm, op_hbm, inn_hbm, field_hbm, courant_hbm,
    sent, to_east, to_west,
    pay, op, inn, strip, meta, tiles, cols, slots, arrived, sems,
):
    blocks = op.shape[0]
    devices = lax.axis_size("lat") * lon_tiles
    parts = 4
    chunk = blocks // parts
    small = [
        pltpu.make_async_copy(a, b, sems.at[k])
        for k, (a, b) in enumerate(
            ((tiles_hbm, tiles), (cols_hbm, cols), (slots_hbm, slots))
        )
    ]
    inn_copy = pltpu.make_async_copy(inn_hbm, inn, sems.at[4])
    copies = []
    for part in range(parts):
        at = pl.ds(part * chunk, chunk)
        copies.append(pltpu.make_async_copy(op_hbm.at[at], op.at[at], sems.at[5 + part]))
    strips = []
    rows = field_hbm.shape[0]
    extra = courant_hbm.shape[0]
    for side, lane_at in enumerate((0, (per_row - 1) * LANE)):
        strips.append(
            pltpu.make_async_copy(
                field_hbm.at[:, pl.ds(lane_at, LANE)], strip.at[side, pl.ds(0, rows)],
                sems.at[5 + parts + 2 * side],
            )
        )
        strips.append(
            pltpu.make_async_copy(
                courant_hbm.at[:, pl.ds(lane_at, LANE)], strip.at[side, pl.ds(rows, extra)],
                sems.at[6 + parts + 2 * side],
            )
        )
    for copy in small + [inn_copy] + copies + strips:
        copy.start()

    def clear(d, _):
        arrived[d] = 0
        meta[pl.ds(aligned(d, 8), 8), :] = jnp.zeros((8, LANE), I32)
        return 0

    lax.fori_loop(0, devices + 1, clear, 0, unroll=8)
    lane8 = lanes8()
    lane = lane8[0:1]
    own = own_group()

    for copy in small:
        copy.wait()
    used = count[0]
    me = lax.axis_index("lat") * lon_tiles + lax.axis_index("lon")
    seat = 8 * (me % 16)
    row_bits = log2_of(per_row)

    def one(j):
        repeat = jnp.where(j < used, 0, 1)
        j = jnp.minimum(j, used - 1)
        dest = tiles[j]
        col = cols[j]
        slot = slots[j]
        nth = jnp.minimum(arrived[dest] - repeat, 1)
        arrived[dest] = nth + 1
        row = col >> row_bits
        at_col = col & (per_row - 1)
        x = jnp.dot(inn[j], op[j], preferred_element_type=F32)
        largest = jnp.max(jnp.abs(x), axis=0, keepdims=True)
        code = jnp.floor(16.0 * jnp.log2(jnp.maximum(largest, 2.0**-100))) + 2.0
        q = jnp.round(x * (1.0 / scale_of(code)))
        pay[dest, pl.ds(pl.multiple_of(nth * LEV, LEV), LEV), :] = q.astype(I32).astype(I16)
        base = aligned(dest, 8)
        meta[pl.ds(base + nth, 1), :] = code.astype(I32)
        rim = (row < slot) | (row >= lat_cells - slot)
        target = (slot * lat_cells + row) * per_row + at_col + 1
        note = jnp.where(lane == seat + 6, 1, target)
        rim_seat = jnp.where(rim, seat + 6, LANE)
        pltpu.store(
            meta.at[pl.ds(base + 5, 1), :], note, mask=(lane == seat + nth) | (lane == rim_seat)
        )
        at_east = at_col == per_row - 1
        near = (at_east | (at_col == 0)) & (slot > 0)
        lon = dest & (lon_tiles - 1)
        other = jnp.where(at_east, lon + 1, lon + lon_tiles - 1) & (lon_tiles - 1)
        beside = jnp.where(near, dest - lon + other, devices)
        piece = nth + jnp.where(at_east, 2, 0)
        first = jnp.where(at_east, LANE - 3, 0)
        offset = jnp.where(at_east, 9, 0) + 4 * nth
        shift = (offset - first) & (LANE - 1)
        wanted = (lane8 >= first) & (lane8 < first + 3)
        mixed = pltpu.roll(jnp.where(wanted, q[:8], 0.0), shift, 1) + pltpu.roll(
            jnp.where(wanted, q[8:], 0.0), (shift + 16) & (LANE - 1), 1
        )
        mixed = jnp.where(own, shared_groups(mixed), 0.0)
        mixed = mixed + pltpu.roll(mixed, 1, 0)
        mixed = (mixed + pltpu.roll(mixed, 2, 0)).astype(I32)
        spot = lane & 15
        here = (spot >= offset) & (spot < offset + 3)
        base = aligned(beside, 8)
        pltpu.store(meta.at[pl.ds(base + 2, 1), :], mixed[3:4], mask=here)
        pltpu.store(meta.at[pl.ds(base + 3, 1), :], mixed[7:8], mask=here)
        turned = pltpu.roll(jnp.broadcast_to(code, (8, LANE)), shift, 1)[0:1].astype(I32)
        pltpu.store(meta.at[pl.ds(base + 4, 1), :], turned, mask=here & (lane < 16))
        note = jnp.where(lane >= seat + 6, 1, slot * lat_cells + row + 1)
        pltpu.store(
            meta.at[pl.ds(base + 5, 1), :], note,
            mask=(lane == seat + 2 + piece) | (lane == seat + 7) | (lane == rim_seat),
        )

    inn_copy.wait()
    for part in range(parts):
        copies[part].wait()

        def some(j, _):
            one(j)
            return 0

        lax.fori_loop(part * chunk, (part + 1) * chunk, some, 0, unroll=32)

    outs = []
    share = devices // parts
    for part in range(parts):

        def settle(d, _):
            pay[d, pl.ds(NOTES, 8), :] = meta[pl.ds(aligned(d, 8), 8), :].astype(I16)
            return 0

        lax.fori_loop(part * share, (part + 1) * share, settle, 0, unroll=share)
        at = pl.ds(part * share, share)
        outs.append(pltpu.make_async_copy(pay.at[at], sent.at[at], sems.at[part]))
        outs[-1].start()
    for copy in strips:
        copy.wait()
    total = (rows + extra) // 8
    for v in range(-(-total // PACK)):
        east = jnp.zeros((8, LANE), F32)
        west = jnp.zeros((8, LANE), F32)
        for k in range(min(PACK, total - v * PACK)):
            at = pl.ds(8 * (v * PACK + k), 8)
            group = lane8 // HALO
            west = jnp.where(group == k, pltpu.roll(strip[0, at, :], HALO * k, 1), west)
            east = jnp.where(group == (k - 1) % PACK, pltpu.roll(strip[1, at, :], HALO * k, 1), east)
        to_east[pl.ds(8 * v, 8), :] = east
        to_west[pl.ds(8 * v, 8), :] = west
    for out in outs:
        out.wait()


def contributions(op_blocks, innovations, obs_tiles, col_blocks, time_slots, obs_count, fields, courant, lat_cells, per_row, lon_tiles, devices):
    blocks = op_blocks.shape[0]
    packed = 8 * -(-(fields.shape[0] + courant.shape[0]) // (8 * PACK))
    strip_rows = fields.shape[0] + courant.shape[0]

    def kernel(*refs):
        contribution_kernel(lat_cells, per_row, lon_tiles, *refs)

    return pl.pallas_call(
        kernel,
        out_shape=[
            pltpu.HBM((devices, ROWS, LANE), I16),
            jax.ShapeDtypeStruct((packed, LANE), F32),
            jax.ShapeDtypeStruct((packed, LANE), F32),
        ],
        in_specs=[pl.BlockSpec(memory_space=pltpu.SMEM)] + [any_spec()] * 7,
        out_specs=[any_spec()] + [vmem_spec()] * 2,
        scratch_shapes=[
            pltpu.VMEM((devices, ROWS, LANE), I16),
            pltpu.VMEM(op_blocks.shape, op_blocks.dtype),
            pltpu.VMEM(innovations.shape, innovations.dtype),
            pltpu.VMEM((2, strip_rows, LANE), F32),
            pltpu.VMEM((8 * (devices + 1), LANE), I32),
            pltpu.SMEM(obs_tiles.shape, I32),
            pltpu.SMEM(col_blocks.shape, I32),
            pltpu.SMEM(time_slots.shape, I32),
            pltpu.SMEM((devices + 1,), I32),
            pltpu.SemaphoreType.DMA((13,)),
        ],
        compiler_params=params(16),
        cost_estimate=pl.CostEstimate(
            flops=2 * blocks * LEV * LANE * LANE, bytes_accessed=6 * 2**20, transcendentals=0
        ),
        name="contributions",
    )(
        obs_count, *map(in_hbm, (obs_tiles, col_blocks, time_slots, op_blocks, innovations, fields, courant))
    )


def ready_kernel(
    lat_cells, per_row, field_hbm, courant_hbm, first_hbm, spread_hbm, lat_hbm,
    first, spread, lat_rows, planes, cplanes, sems,
):
    copies = []
    for c in range(per_row):
        at = pl.ds(c * LANE, LANE)
        copies.append(pltpu.make_async_copy(field_hbm.at[:, at], planes.at[c], sems.at[2 * c]))
        copies.append(pltpu.make_async_copy(courant_hbm.at[:, at], cplanes.at[c], sems.at[2 * c + 1]))
    for copy in copies:
        copy.start()
    for copy in copies:
        copy.wait()

    def widen(g, _):
        for c in range(per_row):
            for d in range(WEIGHTS):
                eight = cplanes[c, pl.ds(pl.multiple_of(d * lat_cells + 8 * g, 8), 8), :]
                for k in range(8):
                    at = pl.ds(pl.multiple_of(((8 * g + k) * WEIGHTS + d) * 8, 8), 8)
                    spread[at, pl.ds(c * LANE, LANE)] = jnp.broadcast_to(eight[k : k + 1], (8, LANE))
        return 0

    lax.fori_loop(0, lat_cells // 8, widen, 0)
    spread_out = pltpu.make_async_copy(spread, spread_hbm.at[:, pl.ds(0, per_row * LANE)], sems.at[0])
    spread_out.start()
    parts = [(h, c) for h in range(LEV // 8) for c in range(per_row)]

    def row_of(i):
        return {
            (h, c): planes[c, pl.ds(8 * h * lat_cells + i, 8, stride=lat_cells), :] for h, c in parts
        }

    def finish(i, total, h, c):
        first[pl.ds(i * LEV + 8 * h, 8), pl.ds(c * LANE, LANE)] = total

    for side, i in enumerate((0, lat_cells - 1)):
        row = row_of(i)
        for h, c in parts:
            lat_rows[pl.ds(LEV * side + 8 * h, 8), pl.ds(c * LANE, LANE)] = row[h, c]
    sweep(lat_cells, per_row + 1, per_row, spread, row_of, None, finish)
    outs = [
        pltpu.make_async_copy(first, first_hbm, sems.at[1]),
        pltpu.make_async_copy(lat_rows, lat_hbm.at[:, pl.ds(0, per_row * LANE)], sems.at[2]),
    ]
    for out in outs:
        out.start()
    for out in outs + [spread_out]:
        out.wait()


def sweep(lat_cells, tiles, given, spread, row_of, force_of, finish, row_done=None):
    lane = lanes8()
    halves = range(LEV // 8)

    def weight_of(i, d):
        at = pl.ds((i * WEIGHTS + d) * 8, 8)
        return [spread[at, pl.ds(c * LANE, LANE)] for c in range(given)]

    def one_row(i, before, mine, after):
        center, east, west, south = (weight_of(i, d) for d in range(4))
        north = weight_of(i + 1, 4) if after is not None else None
        handed = {}
        for h in halves:
            up = [east[c] * mine[h, c] for c in range(given)]
            dn = [west[c] * mine[h, c] for c in range(given)]
            for c in range(tiles):
                if c == given:
                    total = jnp.where(lane == LANE - 1, up[c - 1], 0.0)
                    total = pltpu.roll(total, 1, 1)
                    other = jnp.where(lane == 0, dn[0], 0.0)
                    finish(i, total + pltpu.roll(other, LANE - 1, 1), h, c)
                    continue
                left = 0.0 if given < tiles and c == 0 else up[c - 1]
                right = 0.0 if given < tiles and c == given - 1 else dn[(c + 1) % given]
                total = center[c] * mine[h, c]
                total = total + pltpu.roll(jnp.where(lane == LANE - 1, left, up[c]), 1, 1)
                total = total + pltpu.roll(jnp.where(lane == 0, right, dn[c]), LANE - 1, 1)
                if force_of is not None:
                    total = total + force_of(i, h, c)
                if before is not None:
                    total = total + before[h, c]
                if after is not None:
                    total = total + north[c] * after[h, c]
                finish(i, total, h, c)
            for c in range(given):
                handed[h, c] = south[c] * mine[h, c]
        return handed

    before, mine = None, row_of(0)
    for i in range(lat_cells):
        after = row_of(i + 1) if i + 1 < lat_cells else None
        before = one_row(i, before, mine, after)
        mine = after
        if row_done is not None:
            row_done(i)


def ready(fields, courant, lat_cells, per_row):
    wide = (per_row + 1) * LANE
    lon_cells = per_row * LANE

    def kernel(*refs):
        ready_kernel(lat_cells, per_row, *refs)

    return pl.pallas_call(
        kernel,
        out_shape=[
            pltpu.HBM((lat_cells * LEV, wide), F32),
            pltpu.HBM((lat_cells * WEIGHTS * 8, wide), F32),
            pltpu.HBM((2 * LEV, wide), F32),
        ],
        in_specs=[any_spec()] * 2,
        out_specs=[any_spec()] * 3,
        scratch_shapes=[
            pltpu.VMEM((lat_cells * LEV, wide), F32),
            pltpu.VMEM((lat_cells * WEIGHTS * 8, lon_cells), F32),
            pltpu.VMEM((2 * LEV, lon_cells), F32),
            pltpu.VMEM((per_row, fields.shape[0], LANE), F32),
            pltpu.VMEM((per_row, courant.shape[0], LANE), F32),
            pltpu.SemaphoreType.DMA((2 * per_row,)),
        ],
        compiler_params=params(16),
        cost_estimate=pl.CostEstimate(flops=10**7, bytes_accessed=12 * 2**20, transcendentals=0),
        name="first_step",
    )(in_hbm(fields), in_hbm(courant))


def place_kernel(
    lat_cells, per_row, got, east_halo, west_halo, first_hbm, spread_hbm, lat_hbm,
    force, near, far, lat_rows, spread,
    table_v, wrap_g, wrap_c, pieces, table, listed, sems,
):
    wide = (per_row + 1) * LANE
    lon_cells = per_row * LANE
    sources = got.shape[0]
    row_bits = log2_of(per_row)
    top = (STEPS - 1) * lat_cells
    main = pl.ds(0, lon_cells)
    first_copy = pltpu.make_async_copy(first_hbm, force.at[pl.ds(top * LEV, lat_cells * LEV)], sems.at[0])
    lat_copy = pltpu.make_async_copy(lat_hbm.at[:, main], lat_rows.at[:, main], sems.at[1])
    spread_copy = pltpu.make_async_copy(spread_hbm.at[:, main], spread.at[:, main], sems.at[2])
    for copy in (first_copy, lat_copy, spread_copy):
        copy.start()
    for r in range(sources // 16):

        def gather(s, total, r=r):
            return total + got[16 * r + s, pl.ds(NOTES, 8), :].astype(I32)

        total = lax.fori_loop(0, 16, gather, jnp.zeros((8, LANE), I32), unroll=16)
        table_v[pl.ds(r, 1), :] = total[5:6]
    table_copy = pltpu.make_async_copy(table_v, table, sems.at[3])
    table_copy.start()

    def clear(r, _):
        force[pl.ds(aligned(r, LEV), LEV), :] = jnp.zeros((LEV, wide), F32)
        return 0

    lax.fori_loop(0, top, clear, 0, unroll=4)
    lane8 = lanes8()
    rows = wrap_g.shape[0] // 8
    extra = wrap_c.shape[0] // 8
    for n in range(rows + extra):
        v, k = divmod(n, PACK)
        at = pl.ds(8 * v, 8)
        both = jnp.where(lane8 // HALO == k, east_halo[at, :], west_halo[at, :])
        both = pltpu.roll(both, (-HALO * k) % LANE, 1)
        wrap = jnp.where((lane8 < HALO) | (lane8 >= LANE - HALO), both, 0.0)
        if n < rows:
            wrap_g[pl.ds(8 * n, 8), :] = wrap
        else:
            wrap_c[pl.ds(8 * (n - rows), 8), :] = wrap
    last = pl.ds(lon_cells, LANE)
    for g in range(lat_cells // 8):
        for d in range(WEIGHTS):
            eight = wrap_c[pl.ds(d * lat_cells + 8 * g, 8), :]
            for k in range(8):
                spread[pl.ds(((8 * g + k) * WEIGHTS + d) * 8, 8), last] = jnp.broadcast_to(
                    eight[k : k + 1], (8, LANE)
                )
    own = own_group()
    in_low = lane8 < 3
    in_high = lane8 >= LANE - 3

    def unpack(src, _):
        notes = got[src, pl.ds(NOTES, 8), :].astype(I32).astype(F32)
        base = jnp.broadcast_to(scale_of(notes[4:5]), (8, LANE))
        base = jnp.where(lane8 < 8, base, pltpu.roll(base, LANE - 16, 1))
        q = jnp.where(
            sublanes8() < 4,
            jnp.broadcast_to(notes[2:3], (8, LANE)),
            jnp.broadcast_to(notes[3:4], (8, LANE)),
        )
        q = shared_groups(jnp.where(own, q, 0.0))
        halves = [q * base, pltpu.roll(q, LANE - 16, 1) * base]
        for piece in range(PIECES):
            for h, value in enumerate(halves if piece < 2 else halves[::-1]):
                if piece == 1:
                    value = pltpu.roll(value, LANE - 4, 1)
                if piece == 2:
                    value = pltpu.roll(value, 4, 1)
                value = jnp.where(in_low if piece < 2 else in_high, value, 0.0)
                part = pl.ds(pl.multiple_of((src * PIECES + piece) * LEV, LEV) + 8 * h, 8)
                pieces[part, :] = value
        return 0

    lax.fori_loop(0, sources, unpack, 0, unroll=16)
    first_copy.wait()

    def wrap_row(i, h):
        return wrap_g[pl.ds(8 * h * lat_cells + i, 8, stride=lat_cells), :]

    def weight(i, d):
        return spread[pl.ds(pl.multiple_of((i * WEIGHTS + d) * 8, 8), 8), last]

    def wrap_step(i, carry):
        center, east, west, south_w = (weight(i, d) for d in range(4))
        north_w = jnp.where(i < lat_cells - 1, weight(jnp.minimum(i + 1, lat_cells - 1), 4), 0.0)
        handed = []
        for h in range(LEV // 8):
            before, mine = carry[2 * h], carry[2 * h + 1]
            after = wrap_row(jnp.minimum(i + 1, lat_cells - 1), h)
            up = pltpu.roll(east * mine, 1, 1)
            dn = pltpu.roll(west * mine, LANE - 1, 1)
            at = pl.ds(aligned(top + i, LEV) + 8 * h, 8)
            total = center * mine + before + north_w * after
            total = total + jnp.where(lane8 == 0, 0.0, up) + jnp.where(lane8 == LANE - 1, 0.0, dn)
            force[at, last] = force[at, last] + total
            low = pl.ds(0, LANE)
            force[at, low] = force[at, low] + jnp.where(lane8 == 0, up, 0.0)
            high = pl.ds(lon_cells - LANE, LANE)
            force[at, high] = force[at, high] + jnp.where(lane8 == LANE - 1, dn, 0.0)
            handed += [south_w * mine, after]
        return tuple(handed)

    zero = jnp.zeros((8, LANE), F32)
    lax.fori_loop(0, lat_cells, wrap_step, (zero, wrap_row(0, 0), zero, wrap_row(0, 1)), unroll=64)
    for side, i in enumerate((0, lat_cells - 1)):
        for h in range(LEV // 8):
            lat_rows[pl.ds(LEV * side + 8 * h, 8), last] = wrap_row(i, h)
    table_copy.wait()
    lane8 = lanes8()
    dump = STEPS * lat_cells

    last_lanes = pl.ds(wide - LANE, LANE)
    number = 0
    for src in range(sources):

        def entry(k, src=src):
            return table[src // 16, 8 * (src % 16) + k]

        q = got[src, pl.ds(0, NOTES), :].astype(I32).astype(F32)
        scales = scale_of(got[src, pl.ds(NOTES, 8), :].astype(I32).astype(F32))
        for nth in range(2):
            target = entry(nth)
            col = (target - 1) & (per_row - 1)
            row = jnp.where(target > 0, (target - 1) >> row_bits, dump)
            at = pl.ds(aligned(row, LEV), LEV)
            lanes = pl.ds(aligned(col, LANE), LANE)
            value = q[LEV * nth : LEV * nth + LEV] * scales[nth : nth + 1]
            force[at, lanes] = force[at, lanes] + value
        for piece in range(PIECES):
            target = entry(2 + piece)
            listed[number] = target + ((src * PIECES + piece) << 10)
            number = number + jnp.minimum(target, 1)
    for k in range(8):
        listed[number + k] = dump + 1

    def beside(group, _):
        for k in range(8):
            item = listed[8 * group + k]
            part = pl.ds(aligned(item >> 10, LEV), LEV)
            at = pl.ds(aligned((item & 1023) - 1, LEV), LEV)
            force[at, last_lanes] = force[at, last_lanes] + pieces[part, :]
        return 0

    lax.fori_loop(0, (number + 7) >> 3, beside, 0)
    lat_copy.wait()
    spread_copy.wait()
    odd = lax.axis_index("lat") % 2 == 1

    def hand(at, to_south, to_north):
        near[at, :] = jnp.where(odd, to_north, to_south)
        far[at, :] = jnp.where(odd, to_south, to_north)

    n = 0
    for slot in (3, 2, 1):
        for d in range(slot):
            to_south, to_north = (
                force[pl.ds((slot * lat_cells + i) * LEV, LEV), :] for i in (lat_cells - 1 - d, d)
            )
            hand(pl.ds(LEV * n, LEV), to_south, to_north)
            n += 1
    hand(pl.ds(LEV * n, LEV), lat_rows[pl.ds(LEV, LEV), :], lat_rows[pl.ds(0, LEV), :])
    weight_at = LEV * (n + 1)
    sub = lax.broadcasted_iota(I32, (8, wide), 0)
    for d in range(3):
        both = []
        for i in (lat_cells - 1 - d, d):
            rows = jnp.zeros((8, wide), F32)
            for k in range(WEIGHTS):
                rows = jnp.where(sub == k, spread[pl.ds((i * WEIGHTS + k) * 8, 8), :], rows)
            both.append(rows)
        hand(pl.ds(weight_at + 8 * d, 8), *both)


def place(got, from_east, from_west, first, spread, lat_rows, fields, courant, lat_cells, per_row):
    wide = (per_row + 1) * LANE
    rim = (7 * LEV + 24, wide)

    def kernel(*refs):
        place_kernel(lat_cells, per_row, *refs)

    return pl.pallas_call(
        kernel,
        out_shape=[
            pltpu.VMEM(((STEPS * lat_cells + 1) * LEV, wide), F32),
            jax.ShapeDtypeStruct(rim, F32),
            jax.ShapeDtypeStruct(rim, F32),
            jax.ShapeDtypeStruct(lat_rows.shape, F32),
            pltpu.VMEM(spread.shape, F32),
        ],
        in_specs=[vmem_spec()] * 3 + [any_spec()] * 3,
        out_specs=[vmem_spec()] * 5,
        scratch_shapes=[
            pltpu.VMEM((8, LANE), I32),
            pltpu.VMEM((fields.shape[0], LANE), F32),
            pltpu.VMEM((courant.shape[0], LANE), F32),
            pltpu.VMEM((got.shape[0] * PIECES * LEV, LANE), F32),
            pltpu.SMEM((8, LANE), I32),
            pltpu.SMEM((got.shape[0] * PIECES + 8,), I32),
            pltpu.SemaphoreType.DMA((4,)),
        ],
        compiler_params=params(12),
        cost_estimate=pl.CostEstimate(flops=10**6, bytes_accessed=2 * 2**20, transcendentals=0),
        name="place_blocks",
    )(got, from_east, from_west, in_hbm(first), in_hbm(spread), in_hbm(lat_rows))


def steps_kernel(lat_cells, per_row, before, spread, force, out_hbm, result, sems):
    del before
    tiles = per_row + 1

    writes = []
    lon_cells = per_row * LANE
    out_rows = out_hbm.reshape(LEV, lat_cells, lon_cells)

    def at_of(slot, i, h):
        return pl.ds((slot * lat_cells + i) * LEV + 8 * h, 8)

    for slot in reversed(range(STEPS - 1)):

        def row_of(i, slot=slot):
            return {
                (h, c): force[at_of(slot + 1, i, h), pl.ds(c * LANE, LANE)]
                for h in range(LEV // 8)
                for c in range(tiles)
            }

        def force_of(i, h, c, slot=slot):
            return force[at_of(slot, i, h), pl.ds(c * LANE, LANE)]

        def finish(i, total, h, c, slot=slot):
            if slot or i < 8 or i >= lat_cells - 8:
                force[at_of(slot, i, h), pl.ds(c * LANE, LANE)] = total
            else:
                result[c, pl.ds(8 * h * lat_cells + i, 8, stride=lat_cells), :] = total

        def row_done(i):
            if i % 16 == 7 and i > 8:
                rows = pl.ds(i - 15, 16)
                for c in range(per_row):
                    write = pltpu.make_async_copy(
                        result.at[c].reshape(LEV, lat_cells, LANE).at[:, rows],
                        out_rows.at[:, rows, pl.ds(c * LANE, LANE)],
                        sems.at[len(writes)],
                    )
                    write.start()
                    writes.append(write)

        sweep(
            lat_cells, tiles if slot else per_row, tiles, spread, row_of, force_of, finish,
            None if slot else row_done,
        )
    for write in writes:
        write.wait()


def steps(force, spread, lat_cells, per_row):
    lon_cells = per_row * LANE

    def kernel(*refs):
        steps_kernel(lat_cells, per_row, *refs)

    return pl.pallas_call(
        kernel,
        out_shape=[
            pltpu.VMEM(force.shape, F32),
            jax.ShapeDtypeStruct((LEV * lat_cells, lon_cells), F32),
        ],
        in_specs=[vmem_spec()] * 2,
        out_specs=[vmem_spec(), any_spec()],
        scratch_shapes=[
            pltpu.VMEM((per_row, LEV * lat_cells, LANE), F32),
            pltpu.SemaphoreType.DMA((per_row * (lat_cells // 16),)),
        ],
        input_output_aliases={0: 0},
        compiler_params=params(8),
        cost_estimate=pl.CostEstimate(
            flops=10 * STEPS * LEV * lat_cells * lon_cells, bytes_accessed=10 * 2**20, transcendentals=0
        ),
        name="interior_steps",
    )(force, spread)


def along_row(value, weights):
    wide = value.shape[1]
    return (
        weights[0] * value
        + pltpu.roll(weights[1] * value, 1, 1)
        + pltpu.roll(weights[2] * value, wide - 1, 1)
    )


def rim_kernel(
    lat_cells, per_row, before_hbm, near, far, force, lat_rows, spread, out_hbm, tiles, sems
):
    del before_hbm
    wide = force.shape[1]
    lon_cells = per_row * LANE
    weight_at = 7 * LEV
    writes = []
    odd = lax.axis_index("lat") % 2 == 1
    for side, (outer, inner) in enumerate(((3, 4), (4, 3))):

        def halo(at, side=side):
            one, other = near[at, :], far[at, :]
            return jnp.where(odd, one, other) if side == 0 else jnp.where(odd, other, one)

        def mine(q, side=side):
            return q if side == 0 else lat_cells - 1 - q

        def weight(q, d, halo=halo, mine=mine):
            if q < 0:
                row = halo(pl.ds(weight_at + 8 * (-1 - q), 8))[d : d + 1]
                return jnp.broadcast_to(row, (LEV, wide))
            eight = spread[pl.ds((mine(q) * WEIGHTS + d) * 8, 8), :]
            return jnp.concatenate([eight, eight], axis=0)

        def sent(slot, q, halo=halo):
            first = {3: 0, 2: 3, 1: 5, 4: 6}[slot]
            return halo(pl.ds((first - 1 - q) * LEV, LEV))

        def inside(slot, q, side=side, mine=mine):
            if slot == STEPS:
                return lat_rows[pl.ds(LEV * side, LEV), :]
            return force[pl.ds((slot * lat_cells + mine(q)) * LEV, LEV), :]

        now = {}
        for step in range(1, STEPS + 1):
            slot = STEPS - step
            later = {}
            for q in range(-(STEPS - step), step):
                total = sent(slot, q) if q < 0 else None
                if step > 1 and q in now:
                    term = along_row(now[q], [weight(q, d) for d in range(3)])
                    total = term if total is None else total + term
                if step > 1 and q - 1 in now:
                    term = weight(q - 1, outer) * now[q - 1]
                    total = term if total is None else total + term
                if step == 1 and q == 0:
                    total = weight(-1, outer) * sent(STEPS, -1)
                if step > 1 and q + 1 in now:
                    total = total + weight(q + 1, inner) * now[q + 1]
                if q == -1:
                    total = total + weight(0, inner) * inside(slot + 1, 0)
                later[q] = total
            now = later
        for k in range(8):
            i = k if side == 0 else lat_cells - 8 + k
            row = force[pl.ds(i * LEV, LEV), pl.ds(0, lon_cells)]
            q = k if side == 0 else 7 - k
            if q < STEPS:
                row = row + now[q][:, :lon_cells]
            for c in range(per_row):
                tiles[side, c, pl.ds(k, LEV, stride=8), :] = row[:, c * LANE : (c + 1) * LANE]
        for c in range(per_row):
            write = pltpu.make_async_copy(
                tiles.at[side, c].reshape(LEV, 8, LANE),
                out_hbm.reshape(LEV, lat_cells, lon_cells).at[
                    :, pl.ds(0 if side == 0 else lat_cells - 8, 8), pl.ds(c * LANE, LANE)
                ],
                sems.at[per_row * side + c],
            )
            write.start()
            writes.append(write)
    for write in writes:
        write.wait()


def rim(result, near, far, force, lat_rows, spread, lat_cells, per_row):
    def kernel(*refs):
        rim_kernel(lat_cells, per_row, *refs)

    return pl.pallas_call(
        kernel,
        out_shape=jax.ShapeDtypeStruct(result.shape, F32),
        in_specs=[any_spec()] + [vmem_spec()] * 5,
        out_specs=any_spec(),
        scratch_shapes=[
            pltpu.VMEM((2, per_row, 8 * LEV, LANE), F32),
            pltpu.SemaphoreType.DMA((2 * per_row,)),
        ],
        input_output_aliases={0: 0},
        compiler_params=params(8),
        cost_estimate=pl.CostEstimate(flops=10**6, bytes_accessed=2 * 2**20, transcendentals=0),
        name="rim_rows",
    )(result, near, far, force, lat_rows, spread)


def on_device(
    op_blocks, innovations, obs_tiles, col_blocks, time_slots, obs_count, courant, later_adjoint
):
    lat_tiles = lax.axis_size("lat")
    lon_tiles = lax.axis_size("lon")
    devices = lat_tiles * lon_tiles
    levels, lat_cells, lon_cells = later_adjoint.shape
    per_row = lon_cells // LANE
    fields = later_adjoint.reshape(levels * lat_cells, lon_cells)
    weights = courant.reshape(courant.shape[0] * lat_cells, lon_cells)

    sent, to_east, to_west = contributions(
        op_blocks, innovations, obs_tiles, col_blocks, time_slots, obs_count,
        fields, weights, lat_cells, per_row, lon_tiles, devices,
    )
    eastward = [(i, (i + 1) % lon_tiles) for i in range(lon_tiles)]
    westward = [(j, i) for i, j in eastward]
    from_west = lax.ppermute(to_east, "lon", eastward)
    from_east = lax.ppermute(to_west, "lon", westward)
    got = lax.all_to_all(sent, ("lat", "lon"), split_axis=0, concat_axis=0, tiled=True)
    first, spread, lat_rows = ready(fields, weights, lat_cells, per_row)
    force, near, far, lat_rows, spread = place(
        got, from_east, from_west, first, spread, lat_rows, fields, weights, lat_cells, per_row
    )
    pairs = [(i, i + 1) for i in range(lat_tiles - 1)]
    inner = [pair for i, j in pairs[0::2] for pair in ((i, j), (j, i))]
    outer = [pair for i, j in pairs[1::2] for pair in ((i, j), (j, i))]
    far = lax.ppermute(far, "lat", outer)
    near = lax.ppermute(near, "lat", inner)
    force, result = steps(force, spread, lat_cells, per_row)
    result = rim(result, near, far, force, lat_rows, spread, lat_cells, per_row)
    return result.reshape(levels, lat_cells, lon_cells)


def solution(mesh):
    in_specs = (
        P(("lat", "lon"), None, None),
        P(("lat", "lon"), None, None),
        P(("lat", "lon")),
        P(("lat", "lon")),
        P(("lat", "lon")),
        P(("lat", "lon")),
        P(None, "lat", "lon"),
        P(None, "lat", "lon"),
    )
    out_specs = P(None, "lat", "lon")
    return jax.shard_map(
        on_device, mesh=mesh, in_specs=in_specs, out_specs=out_specs, check_vma=False
    )
```
